512 devices in a mesh: ia: 16 (over z_lo, x, core), ja: 8 (over y), ka: 4 (over z_hi).
Axes of the slice: x: 4, y: 8, z: 8 (z_hi: 4, z_lo: 2; z = z_hi * 2 + z_lo), core: 2. Of those that a mesh axis runs over, the one named last changes fastest.
Arguments:
- tensor: float32 [512, 1024, 512], P('ia', 'ja', 'ka'), may hold values from -200 to 200
- factor_b: float32 [1024, 4, 96], P(('ja', 'ka')), may hold values from -4 to 4
- factor_c: float32 [512, 4, 96], P(('ka', 'ja')), may hold values from -4 to 4
Outputs:
- factor_a: float32 [512, 4, 96], P(('ia', 'ja', 'ka'))
- weights: float32 [4, 96], replicated
The draws below stay inside these ranges and needn't reach their ends.
All inputs are finite; a program needn't handle non-finite values.
Results may differ from the reference program's by a relative error of at most 0.0003.
Values sent between devices are 32-bit elements; how exact they have to be, the bound alone decides.
No kernel may reach another device: no remote copies, remote signals or barrier semaphores. Data moves between devices by JAX's collectives and lax.ppermute only.
A program may use at most 64 MiB of HBM per device.

```python
import math
import jax
import jax.numpy as jnp
from jax import lax

R = 96
STARTS = 4
I = 512
J = 1024
K = 512


def rising(key, count, top):
    places = jnp.arange(count, dtype=jnp.float32) / max(count - 1, 1)
    rough = jax.random.uniform(key, (count,), jnp.float32, 0.7, 1.4)
    return jnp.exp(places * math.log(top)) * rough


def factor_draw(key, count):
    keys = jax.random.split(key, 3)
    base = jax.random.truncated_normal(keys[0], -4.0, 4.0, (count, STARTS, R), jnp.float32)
    top_scale = 10.0
    row_scale = rising(keys[1], count, top_scale)
    col_scale = jnp.exp(jax.random.uniform(keys[2], (STARTS, R), jnp.float32, math.log(0.5), math.log(2.0)))
    return base * row_scale[:, None, None] * col_scale[None] * (0.2157 / math.sqrt(count))


def draw_tensor(key, part):
    keys = jax.random.split(key, 4)
    base = jax.random.truncated_normal(keys[0], -4.0, 4.0, (I, J, K), jnp.float32)
    top_scale = 10.0
    first = rising(keys[1], I, top_scale)
    second = rising(keys[2], J, 3.0)
    third = rising(keys[3], K, 3.0)
    return 0.2 * base * first[:, None, None] * second[None, :, None] * third[None, None, :]


def draw_factor_b(key, part):
    return factor_draw(jax.random.fold_in(key, 11), J)


def draw_factor_c(key, part):
    return factor_draw(jax.random.fold_in(key, 23), K)


def setup_inputs(seed: int = 0) -> dict:
    seeds = jax.random.split(jax.random.key(seed), 4)
    return {
        "tensor": draw_tensor(jax.random.fold_in(seeds[3], 71), 0),
        "factor_b": draw_factor_b(jax.random.fold_in(seeds[3], 71), 0),
        "factor_c": draw_factor_c(jax.random.fold_in(seeds[3], 71), 0),
    }


highest = lax.Precision.HIGHEST

def gram_of(rows):
    return jnp.einsum('jsr,jsq->srq', rows.astype(jnp.float32), rows.astype(jnp.float32), precision=highest, preferred_element_type=jnp.float32)

def solve_normal(rows, gram_b, gram_c):
    columns = []
    for member in range(rows.shape[1]):
        normal_mat = gram_b[member] * gram_c[member]
        factor_l = jnp.linalg.cholesky(normal_mat)
        right_side = rows[:, member, :].T
        lower_sol = lax.linalg.triangular_solve(factor_l, right_side, left_side=True, lower=True)
        upper_sol = lax.linalg.triangular_solve(factor_l, lower_sol, left_side=True, lower=True, transpose_a=True)
        columns.append(upper_sol.T)
    return jnp.stack(columns, axis=1)

def reference(tensor, factor_b, factor_c):
    rows_i, rows_j, rows_k = tensor.shape
    starts, col_count = (factor_b.shape[1], factor_b.shape[2])
    width = starts * col_count
    partial_value = jnp.dot(tensor.reshape(rows_i * rows_j, rows_k).astype(jnp.float32), factor_c.reshape(rows_k, width).astype(jnp.float32), precision=highest, preferred_element_type=jnp.float32).reshape(rows_i, rows_j, width)
    mttkrp = jnp.einsum('ijr,jr->ir', partial_value.astype(jnp.float32), factor_b.reshape(rows_j, width).astype(jnp.float32), precision=highest, preferred_element_type=jnp.float32)
    mttkrp = mttkrp.reshape(rows_i, starts, col_count)
    factor_raw = solve_normal(mttkrp, gram_of(factor_b), gram_of(factor_c))
    squares = lax.optimization_barrier(jnp.sum(factor_raw * factor_raw, axis=0))
    weights = jnp.sqrt(squares / rows_i + 1e-06)
    return (factor_raw / weights[None], weights)
```

```python
import jax
import jax.numpy as jnp
from jax import lax
from jax.experimental import pallas as pl
from jax.experimental.pallas import tpu as pltpu
from jax.sharding import PartitionSpec as P

highest = lax.Precision.HIGHEST
f32 = jnp.float32
bf16 = jnp.bfloat16

R = 96
S = 4
W = S * R
VMEM = pl.BlockSpec(memory_space=pltpu.VMEM)


def dot(a, b, dims, precision=highest):
    return lax.dot_general(a, b, (dims, ((), ())), precision=precision, preferred_element_type=f32)


def lanes(shape):
    return lax.broadcasted_iota(jnp.int32, shape, 1)


def rows(shape):
    return lax.broadcasted_iota(jnp.int32, shape, 0)


def call(body, out, cost=None, scratch=()):
    shapes = [jax.ShapeDtypeStruct(o, f32) for o in out]

    def run(*args):
        return pl.pallas_call(
            body,
            out_shape=shapes,
            in_specs=[VMEM] * len(args),
            out_specs=[VMEM] * len(shapes),
            scratch_shapes=list(scratch),
            compiler_params=pltpu.CompilerParams(vmem_limit_bytes=32 * 1024 * 1024),
            cost_estimate=cost,
        )(*args)

    return run


def prepare(fb_ref, fc_ref, out_ref, z_ref):
    nc = fc_ref.shape[0]
    parts, depth = out_ref.shape[0], z_ref.shape[0] // out_ref.shape[0]
    low = lanes((R, 128)) <= rows((R, 128))
    flat = []
    for s in range(S):
        b = fb_ref[:, s, :]
        c = fc_ref[:, s, :]
        flat.append(c)
        wide_b = jnp.concatenate([b, jnp.zeros((b.shape[0], 128 - R), f32)], axis=1)
        wide_c = jnp.concatenate([c, jnp.zeros((c.shape[0], 128 - R), f32)], axis=1)
        gram_b = dot(b, wide_b, ((0,), (0,)))
        gram_c = dot(c, pltpu.roll(wide_c, 1, 1), ((0,), (0,)))
        z_ref[s * R : (s + 1) * R, :] = jnp.where(low, gram_b, gram_c)
    c_flat = jnp.concatenate(flat, axis=1)
    third = depth // 3
    for p in range(parts):
        out_ref[p, 0:nc, :] = c_flat
        for q in range(3):
            at = p * depth + q * third
            out_ref[p, nc : nc + third, q * 128 : (q + 1) * 128] = z_ref[at : at + third, :]


def middle(got_ref, fb_ref, out_ref, z_ref):
    parts = out_ref.shape[0]
    nb = fb_ref.shape[0]
    peers, third = got_ref.shape[0], z_ref.shape[0] // 3
    nc = got_ref.shape[1] - third
    share = got_ref[0, nc:, :]
    for p in range(1, peers):
        share = share + got_ref[p, nc:, :]
    for q in range(3):
        z_ref[q * third : (q + 1) * third, :] = share[:, q * 128 : (q + 1) * 128]
    b_flat = jnp.concatenate([fb_ref[:, s, :] for s in range(S)], axis=1)
    depth = z_ref.shape[0] // parts
    step = depth // 3
    for p in range(parts):
        out_ref[p, 0:nb, :] = b_flat
        for q in range(3):
            at = p * depth + q * step
            out_ref[p, nb : nb + step, q * 128 : (q + 1) * 128] = z_ref[at : at + step, :]
        out_ref[p, nb + step :, :] = jnp.zeros((out_ref.shape[1] - nb - step, W), f32)


def contract(t_ref, c_got_ref, b_got_ref, out_ref, m_ref):
    ni, nj, nk = t_ref.shape
    nc = nk // c_got_ref.shape[0]
    nb = nj // b_got_ref.shape[0]
    c = jnp.concatenate([c_got_ref[p, 0:nc, :] for p in range(c_got_ref.shape[0])], axis=0)
    b = jnp.concatenate([b_got_ref[p, 0:nb, :] for p in range(b_got_ref.shape[0])], axis=0)
    c_high = c.astype(bf16)
    c_low = (c - c_high.astype(f32)).astype(bf16)
    twice = jnp.concatenate([c_high, c_high], axis=0)
    group = 8
    for at in range(0, ni, group):
        t = t_ref[at : at + group, :, :].reshape(group * nj, nk)
        t_high = t.astype(bf16)
        t_low = (t - t_high.astype(f32)).astype(bf16)
        both = jnp.concatenate([t_high, t_low], axis=1)
        value = dot(both, twice, ((1,), (0,)), None) + dot(t_high, c_low, ((1,), (0,)), None)
        value = value.reshape(group, nj, W) * b[None]
        m_ref[at : at + group, :] = jnp.sum(value, axis=1)
    share = b_got_ref[0, nb : nb + 8, :]
    for p in range(1, b_got_ref.shape[0]):
        share = share + b_got_ref[p, nb : nb + 8, :]
    step = 4
    z = jnp.concatenate([share[0:step, q * 128 : (q + 1) * 128] for q in range(3)], axis=0)
    for p in range(out_ref.shape[0]):
        out_ref[p, 0 : 3 * step, :] = z
    pad = jnp.zeros((ni, 128 - R), f32)
    for s in range(S):
        one = jnp.concatenate([m_ref[:, s * R : (s + 1) * R], pad], axis=1)
        out_ref[:, 3 * step + s, :] = one


def own_row(got_ref, out_ref):
    total = jnp.sum(got_ref[:, 12:16, :], axis=0)
    out_ref[...] = jnp.broadcast_to(total[None], out_ref.shape)


def invert(got_ref, out_ref, z_ref):
    for p in range(got_ref.shape[0]):
        z_ref[12 * p : 12 * (p + 1), :] = got_ref[p, 0:12, :]
    lane, row = lanes((R, 128)), rows((R, 128))
    fill = jnp.zeros((128 - R, 128), f32)
    mats = []
    for s in range(S):
        z = z_ref[s * R : (s + 1) * R, :]
        low = jnp.where(lane <= row, z, 0.0)
        b_up = jnp.concatenate([low, fill], axis=0).T[0:R]
        c_up = pltpu.roll(z, 127, 1)
        up = jnp.where((lane >= row) & (lane < R), b_up * c_up, 0.0)
        strict = jnp.where(lane > row, up, 0.0)
        mats.append(up + jnp.concatenate([strict, fill], axis=0).T[0:R])
    lane1 = lanes((1, 128))
    for k in range(R):
        for s in range(S):
            a = mats[s]
            col = a[:, k : k + 1]
            top = a[k : k + 1, :]
            inv = 1.0 / top[:, k : k + 1]
            scaled = jnp.where(lane1 == k, inv, top * inv)
            here = row[:, 0:1] == k
            col = jnp.where(here, -1.0, col)
            kept = jnp.where((lane == k) | (row == k), 0.0, a)
            mats[s] = kept - col * scaled
    for s in range(S):
        out_ref[s] = mats[s]


def solve(m_ref, own_ref, inv_ref, out_ref, raw_ref):
    squares = []
    for s in range(S):
        inv = inv_ref[s]
        raw = dot(m_ref[:, s, 0:R], inv, ((1,), (0,)))
        squares.append(jnp.sum(raw * raw, axis=0, keepdims=True))
        raw_ref[s : s + 1, :] = dot(own_ref[0, :, 0:R], inv, ((1,), (0,)))[s : s + 1]
    total = jnp.concatenate(squares, axis=0)
    out_ref[...] = jnp.broadcast_to(total[None], out_ref.shape)


def finish_of(row_total):
    def finish(got_ref, raw_ref, fa_ref, w_ref):
        total = jnp.sum(got_ref[...], axis=0)
        weights = jnp.sqrt(total / row_total + 1e-06)
        w_ref[...] = weights[:, 0:R]
        fa_ref[0] = (raw_ref[...] / weights)[:, 0:R]

    return finish


def shards(tensor, factor_b, factor_c):
    ni = tensor.shape[0]
    ia, ja, ka = (lax.axis_size(a) for a in ("ia", "ja", "ka"))
    depth = S * R // ja
    slots_c = call(prepare, [(ja, factor_c.shape[0] + depth // 3, W)], scratch=[pltpu.VMEM((S * R, 128), f32)])(
        factor_b, factor_c
    )[0]
    got_c = lax.all_to_all(slots_c, "ja", 0, 0)
    slots_b = call(middle, [(ka, factor_b.shape[0] + 8, W)], scratch=[pltpu.VMEM((depth, 128), f32)])(got_c, factor_b)[0]
    got_b = lax.all_to_all(slots_b, "ka", 0, 0)
    slots_m = call(contract, [(ja * ka, 16, 128)], scratch=[pltpu.VMEM((ni, W), f32)])(tensor, got_c, got_b)[0]
    got_m = lax.all_to_all(slots_m, ("ja", "ka"), 0, 0)
    own = call(own_row, [(ja * ka, S, 128)])(got_m)[0]
    all_rows = lax.all_to_all(own, ("ja", "ka"), 0, 0)
    cost = pl.CostEstimate(flops=int(1e10), bytes_accessed=int(4e7), transcendentals=0)
    inverse = call(invert, [(S, R, 128)], cost=cost, scratch=[pltpu.VMEM((S * R, 128), f32)])(got_m)[0]
    squares, raw = call(solve, [(ia, S, 128), (S, 128)])(all_rows, own, inverse)
    got_s = lax.all_to_all(squares, "ia", 0, 0)
    return tuple(call(finish_of(ni * ia), [(1, S, R), (S, R)])(got_s, raw))


def solution(mesh):
    in_specs = (P("ia", "ja", "ka"), P(("ja", "ka"), None, None), P(("ka", "ja"), None, None))
    out_specs = (P(("ia", "ja", "ka"), None, None), P())
    return jax.shard_map(shards, mesh=mesh, in_specs=in_specs, out_specs=out_specs, check_vma=False)
```

```python
import jax
import jax.numpy as jnp
from jax import lax
from jax.experimental import pallas as pl
from jax.experimental.pallas import tpu as pltpu
from jax.sharding import PartitionSpec as P

highest = lax.Precision.HIGHEST
f32 = jnp.float32
bf16 = jnp.bfloat16

R = 96
S = 4
W = S * R
VMEM = pl.BlockSpec(memory_space=pltpu.VMEM)


def dot(a, b, dims, precision=highest):
    return lax.dot_general(a, b, (dims, ((), ())), precision=precision, preferred_element_type=f32)


def lanes(shape):
    return lax.broadcasted_iota(jnp.int32, shape, 1)


def rows(shape):
    return lax.broadcasted_iota(jnp.int32, shape, 0)


def call(body, out, cost=None, scratch=()):
    shapes = [jax.ShapeDtypeStruct(o, f32) for o in out]

    def run(*args):
        return pl.pallas_call(
            body,
            out_shape=shapes,
            in_specs=[VMEM] * len(args),
            out_specs=[VMEM] * len(shapes),
            scratch_shapes=list(scratch),
            compiler_params=pltpu.CompilerParams(vmem_limit_bytes=32 * 1024 * 1024),
            cost_estimate=cost,
        )(*args)

    return run


def work(flops, nbytes):
    return pl.CostEstimate(flops=int(flops), bytes_accessed=int(nbytes), transcendentals=0)


def prepare(fb_ref, fc_ref, out_ref, b_ref, z_ref):
    nc = fc_ref.shape[0]
    parts, depth = out_ref.shape[0], z_ref.shape[0] // out_ref.shape[0]
    low = lanes((R, 128)) <= rows((R, 128))
    flat = []
    b_ref[...] = jnp.concatenate([fb_ref[:, s, :] for s in range(S)], axis=1)
    for s in range(S):
        b = fb_ref[:, s, :]
        c = fc_ref[:, s, :]
        flat.append(c)
        wide_b = jnp.concatenate([b, jnp.zeros((b.shape[0], 128 - R), f32)], axis=1)
        wide_c = jnp.concatenate([c, jnp.zeros((c.shape[0], 128 - R), f32)], axis=1)
        gram_b = dot(b, wide_b, ((0,), (0,)))
        gram_c = dot(c, pltpu.roll(wide_c, 1, 1), ((0,), (0,)))
        z_ref[s * R : (s + 1) * R, :] = jnp.where(low, gram_b, gram_c)
    c_flat = jnp.concatenate(flat, axis=1)
    third = depth // 3
    for p in range(parts):
        out_ref[p, 0:nc, :] = c_flat
        for q in range(3):
            at = p * depth + q * third
            out_ref[p, nc : nc + third, q * 128 : (q + 1) * 128] = z_ref[at : at + third, :]


def middle(got_ref, out_ref, z_ref):
    parts = out_ref.shape[0]
    peers, third = got_ref.shape[0], z_ref.shape[0] // 3
    nc = got_ref.shape[1] - third
    share = got_ref[0, nc:, :]
    for p in range(1, peers):
        share = share + got_ref[p, nc:, :]
    for q in range(3):
        z_ref[q * third : (q + 1) * third, :] = share[:, q * 128 : (q + 1) * 128]
    step = z_ref.shape[0] // parts
    for p in range(parts):
        out_ref[p, 0:step, :] = z_ref[p * step : (p + 1) * step, :]
        out_ref[p, step:, :] = jnp.zeros((out_ref.shape[1] - step, 128), f32)


def contract(t_ref, c_got_ref, b_ref, out_ref):
    ni, nj, nk = t_ref.shape
    nc = nk // c_got_ref.shape[0]
    c = jnp.concatenate([c_got_ref[p, 0:nc, :] for p in range(c_got_ref.shape[0])], axis=0)
    b = b_ref[...]
    c_high = c.astype(bf16)
    c_low = (c - c_high.astype(f32)).astype(bf16)
    twice = jnp.concatenate([c_high, c_high], axis=0)
    group = 8
    for at in range(0, ni, group):
        t = t_ref[at : at + group, :, :].reshape(group * nj, nk)
        t_high = t.astype(bf16)
        t_low = (t - t_high.astype(f32)).astype(bf16)
        both = jnp.concatenate([t_high, t_low], axis=1)
        value = dot(both, twice, ((1,), (0,)), None) + dot(t_high, c_low, ((1,), (0,)), None)
        value = value.reshape(group, nj, W) * b[None]
        out_ref[at : at + group, :] = jnp.sum(value, axis=1)


def pack(m_ref, z_got_ref, out_ref):
    share = jnp.sum(z_got_ref[...], axis=0)
    out_ref[:, 0:12, :] = jnp.broadcast_to(share[None, 0:12], (out_ref.shape[0], 12, 128))
    pad = jnp.zeros((m_ref.shape[0], 128 - R), f32)
    for s in range(S):
        one = jnp.concatenate([m_ref[:, s * R : (s + 1) * R], pad], axis=1)
        out_ref[:, 12 + s, :] = one


def own_row(got_ref, out_ref):
    total = jnp.sum(got_ref[:, 12:16, :], axis=0)
    out_ref[...] = jnp.broadcast_to(total[None], out_ref.shape)


def invert(got_ref, out_ref, z_ref):
    for p in range(got_ref.shape[0]):
        z_ref[12 * p : 12 * (p + 1), :] = got_ref[p, 0:12, :]
    lane, row = lanes((R, 128)), rows((R, 128))
    fill = jnp.zeros((128 - R, 128), f32)
    mats = []
    for s in range(S):
        z = z_ref[s * R : (s + 1) * R, :]
        low = jnp.where(lane <= row, z, 0.0)
        b_up = jnp.concatenate([low, fill], axis=0).T[0:R]
        c_up = pltpu.roll(z, 127, 1)
        up = jnp.where((lane >= row) & (lane < R), b_up * c_up, 0.0)
        strict = jnp.where(lane > row, up, 0.0)
        mats.append(up + jnp.concatenate([strict, fill], axis=0).T[0:R])
    lane1, lane8, row8 = lanes((1, 128)), lanes((8, 128)), rows((8, 1))
    count = R // 8
    blocks = [[mats[s][8 * i : 8 * i + 8] for i in range(count)] for s in range(S)]
    scale = [jnp.zeros((1, 128), f32)] * S
    for k in range(R):
        own, at = divmod(k, 8)
        for s in range(S):
            top = blocks[s][own][at : at + 1]
            inv = 1.0 / jnp.broadcast_to(top[:, k : k + 1], (1, 128))
            scale[s] = jnp.where(lane1 == k, inv, scale[s])
            full = jnp.broadcast_to(jnp.where(lane1 == k, 1.0, top) * inv, (8, 128))
            for i in range(own if at < 7 else own + 1, count):
                a = blocks[s][i]
                new = jnp.where(lane8 == k, 0.0, a) - a[:, k : k + 1] * full
                blocks[s][i] = jnp.where(row8 > at, new, a) if i == own else new
    for s in range(S):
        w = jnp.concatenate(blocks[s], axis=0)
        w = jnp.where(lane == row, 1.0, jnp.where(lane < row, w, 0.0))
        inv = jnp.sum(jnp.where(lane == row, scale[s], 0.0), axis=1, keepdims=True)
        out_ref[s] = dot(w[:, 0:R], w * inv, ((0,), (0,)))


def solve(m_ref, own_ref, inv_ref, out_ref, raw_ref):
    squares = []
    for s in range(S):
        inv = inv_ref[s]
        raw = dot(m_ref[:, s, 0:R], inv, ((1,), (0,)))
        squares.append(jnp.sum(raw * raw, axis=0, keepdims=True))
        raw_ref[s : s + 1, :] = dot(own_ref[0, :, 0:R], inv, ((1,), (0,)))[s : s + 1]
    total = jnp.concatenate(squares, axis=0)
    out_ref[...] = jnp.broadcast_to(total[None], out_ref.shape)


def finish_of(row_total):
    def finish(got_ref, raw_ref, fa_ref, w_ref):
        total = jnp.sum(got_ref[...], axis=0)
        weights = jnp.sqrt(total / row_total + 1e-06)
        w_ref[...] = weights[:, 0:R]
        fa_ref[0] = (raw_ref[...] / weights)[:, 0:R]

    return finish


def shards(tensor, factor_b, factor_c):
    ni = tensor.shape[0]
    ia, ja, ka = (lax.axis_size(a) for a in ("ia", "ja", "ka"))
    depth = S * R // ja
    nb, nc = factor_b.shape[0], factor_c.shape[0]
    slots_c, b_flat = call(prepare, [(ja, nc + depth // 3, W), (nb, W)], scratch=[pltpu.VMEM((S * R, 128), f32)])(
        factor_b, factor_c
    )
    got_c = lax.all_to_all(slots_c, "ja", 0, 0)
    b_block = lax.all_gather(b_flat, "ka", axis=0, tiled=True)
    slots_z = call(middle, [(ka, 16, 128)], scratch=[pltpu.VMEM((depth, 128), f32)])(got_c)[0]
    got_z = lax.all_to_all(slots_z, "ka", 0, 0)
    m_part = call(contract, [(ni, W)], cost=work(2e9, 4e6))(tensor, got_c, b_block)[0]
    slots_m = call(pack, [(ja * ka, 16, 128)])(m_part, got_z)[0]
    got_m = lax.all_to_all(slots_m, ("ja", "ka"), 0, 0)
    own = call(own_row, [(ja * ka, S, 128)])(got_m)[0]
    all_rows = lax.all_to_all(own, ("ja", "ka"), 0, 0)
    inverse = call(invert, [(S, R, 128)], cost=work(1e10, 4e7), scratch=[pltpu.VMEM((S * R, 128), f32)])(got_m)[0]
    squares, raw = call(solve, [(ia, S, 128), (S, 128)])(all_rows, own, inverse)
    got_s = lax.all_to_all(squares, "ia", 0, 0)
    return tuple(call(finish_of(ni * ia), [(1, S, R), (S, R)])(got_s, raw))


def solution(mesh):
    in_specs = (P("ia", "ja", "ka"), P(("ja", "ka"), None, None), P(("ka", "ja"), None, None))
    out_specs = (P(("ia", "ja", "ka"), None, None), P())
    return jax.shard_map(shards, mesh=mesh, in_specs=in_specs, out_specs=out_specs, check_vma=False)
```

```python
import jax
import jax.numpy as jnp
from jax import lax
from jax.experimental import pallas as pl
from jax.experimental.pallas import tpu as pltpu
from jax.sharding import PartitionSpec as P

highest = lax.Precision.HIGHEST
f32 = jnp.float32
bf16 = jnp.bfloat16

R = 96
S = 4
W = S * R
VMEM = pl.BlockSpec(memory_space=pltpu.VMEM)
HBM = pl.BlockSpec(memory_space=pltpu.HBM)


def dot(a, b, dims, precision=highest):
    return lax.dot_general(a, b, (dims, ((), ())), precision=precision, preferred_element_type=f32)


def lanes(shape):
    return lax.broadcasted_iota(jnp.int32, shape, 1)


def rows(shape):
    return lax.broadcasted_iota(jnp.int32, shape, 0)


def call(body, out, cost=None, scratch=(), hbm=0, limit=32):
    shapes = [jax.ShapeDtypeStruct(o, f32) for o in out]

    def run(*args):
        return pl.pallas_call(
            body,
            out_shape=shapes,
            in_specs=[HBM] * hbm + [VMEM] * (len(args) - hbm),
            out_specs=[VMEM] * len(shapes),
            scratch_shapes=list(scratch),
            compiler_params=pltpu.CompilerParams(vmem_limit_bytes=limit * 1024 * 1024),
            cost_estimate=cost,
        )(*args)

    return run


def work(flops, nbytes):
    return pl.CostEstimate(flops=int(flops), bytes_accessed=int(nbytes), transcendentals=0)


def prepare(fb_hbm, fc_hbm, out_ref, b_ref, z_ref, fb_ref, fc_ref, sems):
    copy_c = pltpu.make_async_copy(fc_hbm, fc_ref, sems.at[0])
    copy_b = pltpu.make_async_copy(fb_hbm, fb_ref, sems.at[1])
    copy_c.start()
    copy_b.start()
    copy_c.wait()
    c_flat = jnp.concatenate([fc_ref[:, s, :] for s in range(S)], axis=1)
    out_ref[...] = jnp.broadcast_to(c_flat[None], out_ref.shape)
    copy_b.wait()
    b_ref[...] = jnp.concatenate([fb_ref[:, s, :] for s in range(S)], axis=1)
    low = lanes((R, 128)) <= rows((R, 128))
    for s in range(S):
        b = fb_ref[:, s, :]
        c = fc_ref[:, s, :]
        wide_b = jnp.concatenate([b, jnp.zeros((b.shape[0], 128 - R), f32)], axis=1)
        wide_c = jnp.concatenate([c, jnp.zeros((c.shape[0], 128 - R), f32)], axis=1)
        gram_b = dot(b, wide_b, ((0,), (0,)))
        gram_c = dot(c, pltpu.roll(wide_c, 1, 1), ((0,), (0,)))
        z_ref[s * R : (s + 1) * R, :] = jnp.where(low, gram_b, gram_c)


def contract(t_hbm, z_hbm, c_ref, b_ref, out_ref, t_ref, z_ref, m_ref, sems):
    ni, nj, nk = t_ref.shape
    steps = sems.shape[0] - 1
    group = ni // steps
    copy_z = pltpu.make_async_copy(z_hbm, z_ref, sems.at[steps])
    parts = [pl.ds(n * group, group) for n in range(steps)]
    copies = [pltpu.make_async_copy(t_hbm.at[p], t_ref.at[p], sems.at[n]) for n, p in enumerate(parts)]
    for copy in copies + [copy_z]:
        copy.start()
    c = c_ref[...].reshape(nk, W)
    c_high = c.astype(bf16)
    c_low = (c - c_high.astype(f32)).astype(bf16)
    twice = jnp.concatenate([c_high, c_high], axis=0)
    b = b_ref[...]
    for n in range(steps):
        copies[n].wait()
        at = n * group
        t = t_ref[at : at + group, :, :].reshape(group * nj, nk)
        t_high = t.astype(bf16)
        t_low = (t - t_high.astype(f32)).astype(bf16)
        both = jnp.concatenate([t_high, t_low], axis=1)
        value = dot(both, twice, ((1,), (0,)), None) + dot(t_high, c_low, ((1,), (0,)), None)
        value = value.reshape(group, nj, W) * b[None]
        m_ref[at : at + group, :] = jnp.sum(value, axis=1)
    copy_z.wait()
    for p in range(ni):
        out_ref[p, 0:12, :] = z_ref[12 * p : 12 * (p + 1), :]
    out_ref[:, 15, :] = jnp.zeros((ni, 128), f32)
    for q in range(3):
        out_ref[:, 12 + q, :] = m_ref[:, q * 128 : (q + 1) * 128]


def total(got_ref, out_ref):
    out_ref[...] = jnp.broadcast_to(jnp.sum(got_ref[...], axis=0)[None], out_ref.shape)


def block(got_ref, out_ref):
    flat = jnp.concatenate([got_ref[:, 12 + q, :] for q in range(3)], axis=1)
    out_ref[...] = jnp.broadcast_to(flat[None], out_ref.shape)


def invert(got_ref, own_ref, out_ref, raw_ref, z_ref):
    for p in range(got_ref.shape[0]):
        z_ref[12 * p : 12 * (p + 1), :] = got_ref[p, 0:12, :]
    lane, row = lanes((R, 128)), rows((R, 128))
    fill = jnp.zeros((128 - R, 128), f32)
    mats = []
    for s in range(S):
        z = z_ref[s * R : (s + 1) * R, :]
        low = jnp.where(lane <= row, z, 0.0)
        b_up = jnp.concatenate([low, fill], axis=0).T[0:R]
        c_up = pltpu.roll(z, 127, 1)
        up = jnp.where((lane >= row) & (lane < R), b_up * c_up, 0.0)
        strict = jnp.where(lane > row, up, 0.0)
        mats.append(up + jnp.concatenate([strict, fill], axis=0).T[0:R])
    lane1, lane8, row8 = lanes((1, 128)), lanes((8, 128)), rows((8, 1))
    count = R // 8
    blocks = [[mats[s][8 * i : 8 * i + 8] for i in range(count)] for s in range(S)]
    scale = [jnp.zeros((1, 128), f32)] * S
    for k in range(R):
        own, at = divmod(k, 8)
        for s in range(S):
            top = blocks[s][own][at : at + 1]
            inv = 1.0 / jnp.broadcast_to(top[:, k : k + 1], (1, 128))
            scale[s] = jnp.where(lane1 == k, inv, scale[s])
            full = jnp.broadcast_to(jnp.where(lane1 == k, 1.0, top) * inv, (8, 128))
            for i in range(own if at < 7 else own + 1, count):
                a = blocks[s][i]
                new = jnp.where(lane8 == k, 0.0, a) - a[:, k : k + 1] * full
                blocks[s][i] = jnp.where(row8 > at, new, a) if i == own else new
    for s in range(S):
        w = jnp.concatenate(blocks[s], axis=0)
        w = jnp.where(lane == row, 1.0, jnp.where(lane < row, w, 0.0))
        inv = jnp.sum(jnp.where(lane == row, scale[s], 0.0), axis=1, keepdims=True)
        inverse = dot(w[:, 0:R], w * inv, ((0,), (0,)))[:, 0:R]
        sides = [jnp.zeros((R, n * R), f32) for n in (s, S - 1 - s) if n]
        parts = [inverse] + sides if s == 0 else sides[:1] + [inverse] + sides[1:]
        out_ref[s * R : (s + 1) * R, :] = jnp.concatenate(parts, axis=1)
    row_own = jnp.concatenate([own_ref[0, 12 + q : 13 + q, :] for q in range(3)], axis=1)
    raw_ref[...] = dot(row_own, out_ref[...], ((1,), (0,)))


def finish(m_ref, inv_ref, raw_ref, fa_ref, w_ref):
    count = m_ref.shape[0] * m_ref.shape[1]
    raw = dot(m_ref[...].reshape(count, W), inv_ref[...], ((1,), (0,)))
    squares = jnp.sum(raw * raw, axis=0, keepdims=True)
    weights = jnp.sqrt(squares / count + 1e-06)
    scaled = raw_ref[...] / weights
    for s in range(S):
        fa_ref[0, s : s + 1, :] = scaled[:, s * R : (s + 1) * R]
        w_ref[s : s + 1, :] = weights[:, s * R : (s + 1) * R]


def shards(tensor, factor_b, factor_c):
    ni = tensor.shape[0]
    ia, ja, ka = (lax.axis_size(a) for a in ("ia", "ja", "ka"))
    nb, nc = factor_b.shape[0], factor_c.shape[0]
    slots_c, b_flat, share = call(
        prepare,
        [(ja, nc, W), (nb, W), (S * R, 128)],
        scratch=[pltpu.VMEM(factor_b.shape, f32), pltpu.VMEM(factor_c.shape, f32), pltpu.SemaphoreType.DMA((2,))],
        hbm=2,
        limit=56,
    )(factor_b, factor_c)
    got_c = lax.all_to_all(slots_c, "ja", 0, 0)
    b_block = lax.all_gather(b_flat, "ka", axis=0, tiled=True)
    slots_m = call(
        contract,
        [(ja * ka, 16, 128)],
        scratch=[pltpu.VMEM(v, f32) for v in (tensor.shape, share.shape, (ni, W))] + [pltpu.SemaphoreType.DMA((5,))],
        hbm=2,
        limit=52,
    )(tensor, share, got_c, b_block)[0]
    got_m = lax.all_to_all(slots_m, ("ja", "ka"), 0, 0)
    own = call(total, [(ja * ka, 16, 128)])(got_m)[0]
    got_all = lax.all_to_all(own, ("ja", "ka"), 0, 0)
    slots_i = call(block, [(ia, ni, W)])(got_all)[0]
    m_all = lax.all_to_all(slots_i, "ia", 0, 0)
    inverse, raw = call(invert, [(W, W), (1, W)], cost=work(1e10, 4e7), scratch=[pltpu.VMEM((S * R, 128), f32)])(
        got_all, own
    )
    return tuple(call(finish, [(1, S, R), (S, R)])(m_all, inverse, raw))


def solution(mesh):
    in_specs = (P("ia", "ja", "ka"), P(("ja", "ka"), None, None), P(("ka", "ja"), None, None))
    out_specs = (P(("ia", "ja", "ka"), None, None), P())
    return jax.shard_map(shards, mesh=mesh, in_specs=in_specs, out_specs=out_specs, check_vma=False)
```

```python
import jax
import jax.numpy as jnp
from jax import lax
from jax.experimental import pallas as pl
from jax.experimental.pallas import tpu as pltpu
from jax.sharding import PartitionSpec as P

highest = lax.Precision.HIGHEST
f32 = jnp.float32
bf16 = jnp.bfloat16

R = 96
S = 4
W = S * R
VMEM = pl.BlockSpec(memory_space=pltpu.VMEM)
HBM = pl.BlockSpec(memory_space=pltpu.HBM)


def dot(a, b, dims, precision=highest):
    return lax.dot_general(a, b, (dims, ((), ())), precision=precision, preferred_element_type=f32)


def lanes(shape):
    return lax.broadcasted_iota(jnp.int32, shape, 1)


def rows(shape):
    return lax.broadcasted_iota(jnp.int32, shape, 0)


def call(body, out, cost=None, scratch=(), hbm=0, limit=32):
    shapes = [jax.ShapeDtypeStruct(o, f32) for o in out]

    def run(*args):
        return pl.pallas_call(
            body,
            out_shape=shapes,
            in_specs=[HBM] * hbm + [VMEM] * (len(args) - hbm),
            out_specs=[VMEM] * len(shapes),
            scratch_shapes=list(scratch),
            compiler_params=pltpu.CompilerParams(vmem_limit_bytes=limit * 1024 * 1024),
            cost_estimate=cost,
        )(*args)

    return run


def prepare(fb_hbm, fc_hbm, out_ref, b_ref, z_ref, fb_ref, fc_ref, sems):
    copy_c = pltpu.make_async_copy(fc_hbm, fc_ref, sems.at[0])
    copy_b = pltpu.make_async_copy(fb_hbm, fb_ref, sems.at[1])
    copy_c.start()
    copy_b.start()
    copy_c.wait()
    parts, nc = out_ref.shape[0], fc_ref.shape[0]
    third = S * R // parts // 3
    c_flat = jnp.concatenate([fc_ref[:, s, :] for s in range(S)], axis=1)
    for p in range(parts):
        out_ref[p, 0:nc, :] = c_flat
    copy_b.wait()
    b_ref[...] = jnp.concatenate([fb_ref[:, s, :] for s in range(S)], axis=1)
    low = lanes((R, 128)) <= rows((R, 128))
    for s in range(S):
        b = fb_ref[:, s, :]
        c = fc_ref[:, s, :]
        wide_b = jnp.concatenate([b, jnp.zeros((b.shape[0], 128 - R), f32)], axis=1)
        wide_c = jnp.concatenate([c, jnp.zeros((c.shape[0], 128 - R), f32)], axis=1)
        gram_b = dot(b, wide_b, ((0,), (0,)))
        gram_c = dot(c, pltpu.roll(wide_c, 1, 1), ((0,), (0,)))
        z_ref[s * R : (s + 1) * R, :] = jnp.where(low, gram_b, gram_c)
    for p in range(parts):
        for q in range(3):
            at = (3 * p + q) * third
            out_ref[p, nc : nc + third, q * 128 : (q + 1) * 128] = z_ref[at : at + third, :]


def contract(t_hbm, c_got_ref, b_ref, out_ref, share_ref, t_ref, sems):
    ni, nj, nk = t_ref.shape
    steps = sems.shape[0]
    group = ni // steps
    parts = [pl.ds(n * group, group) for n in range(steps)]
    copies = [pltpu.make_async_copy(t_hbm.at[p], t_ref.at[p], sems.at[n]) for n, p in enumerate(parts)]
    for copy in copies:
        copy.start()
    nc = nk // c_got_ref.shape[0]
    share_ref[...] = jnp.sum(c_got_ref[:, nc:, :], axis=0)
    c = c_got_ref[:, 0:nc, :].reshape(nk, W)
    b = b_ref[...]
    c_high = c.astype(bf16)
    c_low = (c - c_high.astype(f32)).astype(bf16)
    twice = jnp.concatenate([c_high, c_high], axis=0)
    each = out_ref.shape[1]
    for n in range(steps):
        copies[n].wait()
        at = n * group
        t = t_ref[at : at + group, :, :].reshape(group * nj, nk)
        t_high = t.astype(bf16)
        t_low = (t - t_high.astype(f32)).astype(bf16)
        both = jnp.concatenate([t_high, t_low], axis=1)
        value = dot(both, twice, ((1,), (0,)), None) + dot(t_high, c_low, ((1,), (0,)), None)
        value = jnp.sum(value.reshape(group, nj, W) * b[None], axis=1)
        for p in range(group // each):
            out_ref[at // each + p] = value[p * each : (p + 1) * each]


def mix(m_ref, share_ref, out_ref):
    depth, each = share_ref.shape[0], m_ref.shape[1]
    out_ref[0:depth, :] = share_ref[...]
    out_ref[depth : depth + each, :] = jnp.sum(m_ref[...], axis=0)
    out_ref[depth + each :, :] = jnp.zeros((out_ref.shape[0] - depth - each, W), f32)


def spread(x_ref, out_ref):
    out_ref[...] = jnp.broadcast_to(x_ref[...][None], out_ref.shape)


def wide(v):
    return jnp.broadcast_to(v, (8, 128))


def eliminate(blocks, scale, k, q, lane8, row8):
    own, m = divmod(k, 8)
    hit = (lane8 >= k) & (lane8 < k + q)
    mine = blocks[own]
    row = [wide(mine[m + p : m + p + 1]) for p in range(q)]
    cols = [wide(mine[:, k + j : k + j + 1]) for j in range(q)]
    a = {(p, j): wide(cols[j][m + p : m + p + 1]) for p in range(q) for j in range(p, q)}
    inv, u, unit = [], {}, []
    for p in range(q):
        inv.append(1.0 / a[p, p])
        unit.append(jnp.where(lane8 == k + p, 1.0, row[p]))
        scale = jnp.where(lane8 == k + p, inv[p], scale)
        for i in range(p + 1, q):
            u[i, p] = a[p, i] * inv[p]
            for j in range(i, q):
                a[i, j] = a[i, j] - u[i, p] * a[p, j]
        for i in range(p + 1, q):
            row[i] = jnp.where(lane8 == k + p, 0.0, row[i]) - u[i, p] * unit[p]
    steps = [None] * q
    for p in reversed(range(q)):
        step = jnp.where((lane8 > k + p) & hit, 0.0, unit[p]) * inv[p]
        for j in range(p + 1, q):
            step = step - u[j, p] * steps[j]
        steps[p] = step
    for i in range(own, len(blocks)):
        old = blocks[i]
        new = jnp.where(hit, 0.0, old)
        for p in range(q):
            new = new - wide(old[:, k + p : k + p + 1]) * steps[p]
        if i == own:
            new = jnp.where(row8 >= m + q, new, old)
            for p in range(1, q):
                new = jnp.where(row8 == m + p, row[p], new)
        blocks[i] = new
    return scale


def solve(got_ref, own_ref, out_ref, raw_ref, z_ref, m_ref):
    peers = got_ref.shape[0]
    third = S * R // peers // 3
    each = m_ref.shape[0] // peers - 1
    for p in range(peers):
        m_ref[each * p : each * (p + 1), :] = got_ref[p, third : third + each, :]
        for q in range(3):
            at = (3 * p + q) * third
            z_ref[at : at + third, :] = got_ref[p, 0:third, q * 128 : (q + 1) * 128]
    count = each * peers
    mine = own_ref[pl.ds(third + lax.axis_index("ka"), 1), :]
    m_ref[count:, :] = jnp.broadcast_to(mine, (m_ref.shape[0] - count, W))
    lane, row = lanes((R, 128)), rows((R, 128))
    fill = jnp.zeros((128 - R, 128), f32)
    blocks = []
    for s in range(S):
        z = z_ref[s * R : (s + 1) * R, :]
        low = jnp.where(lane <= row, z, 0.0)
        b_up = jnp.concatenate([low, fill], axis=0).T[0:R]
        c_up = pltpu.roll(z, 127, 1)
        up = jnp.where((lane >= row) & (lane < R), b_up * c_up, 0.0)
        strict = jnp.where(lane > row, up, 0.0)
        full = up + jnp.concatenate([strict, fill], axis=0).T[0:R]
        blocks.append([full[8 * i : 8 * i + 8] for i in range(R // 8)])
    lane8, row8 = lanes((8, 128)), rows((8, 1))
    scale = [jnp.zeros((8, 128), f32)] * S
    for k in range(0, R, 4):
        for s in range(S):
            scale[s] = eliminate(blocks[s], scale[s], k, 4, lane8, row8)
    squares = []
    for s in range(S):
        w = jnp.concatenate(blocks[s], axis=0)
        w = jnp.where(lane == row, 1.0, jnp.where(lane < row, w, 0.0))
        half = dot(m_ref[:, s * R : (s + 1) * R], w[:, 0:R], ((1,), (1,))) * scale[s][0:1, 0:R]
        raw = dot(half, w, ((1,), (0,)))
        squares.append(jnp.sum(raw[0:count] * raw[0:count], axis=0, keepdims=True))
        raw_ref[s : s + 1, :] = raw[count : count + 1]
    out_ref[...] = jnp.broadcast_to(jnp.concatenate(squares, axis=0)[None], out_ref.shape)


def finish_of(row_total):
    def finish(got_ref, raw_ref, fa_ref, w_ref):
        total = jnp.sum(got_ref[...], axis=0)
        weights = jnp.sqrt(total / row_total + 1e-06)
        w_ref[...] = weights[:, 0:R]
        fa_ref[0] = (raw_ref[...] / weights)[:, 0:R]

    return finish


def shards(tensor, factor_b, factor_c):
    ni = tensor.shape[0]
    ia, ja, ka = (lax.axis_size(a) for a in ("ia", "ja", "ka"))
    nb, nc = factor_b.shape[0], factor_c.shape[0]
    third = S * R // ja // 3
    each = ni // ja
    grams = pltpu.VMEM((S * R, 128), f32)
    slots_c, b_flat = call(
        prepare,
        [(ja, nc + third, W), (nb, W)],
        scratch=[grams, pltpu.VMEM(factor_b.shape, f32), pltpu.VMEM(factor_c.shape, f32), pltpu.SemaphoreType.DMA((2,))],
        hbm=2,
        limit=56,
    )(factor_b, factor_c)
    got_c = lax.all_to_all(slots_c, "ja", 0, 0)
    b_block = lax.all_gather(b_flat, "ka", axis=0, tiled=True)
    slots_m, share = call(
        contract,
        [(ja, each, W), (third, W)],
        scratch=[pltpu.VMEM(tensor.shape, f32), pltpu.SemaphoreType.DMA((4,))],
        hbm=1,
        limit=52,
    )(tensor, got_c, b_block)
    got_m = lax.all_to_all(slots_m, "ja", 0, 0)
    sums = lax.psum(call(mix, [(third + 8, W)])(got_m, share)[0], "ka")
    got_all = lax.all_to_all(call(spread, [(ja, third + 8, W)])(sums)[0], "ja", 0, 0)
    squares, raw = call(solve, [(ia, S, 128), (S, 128)], scratch=[grams, pltpu.VMEM((ni + ja, W), f32)])(got_all, sums)
    got_s = lax.all_to_all(squares, "ia", 0, 0)
    return tuple(call(finish_of(ni * ia), [(1, S, R), (S, R)])(got_s, raw))


def solution(mesh):
    in_specs = (P("ia", "ja", "ka"), P(("ja", "ka"), None, None), P(("ka", "ja"), None, None))
    out_specs = (P(("ia", "ja", "ka"), None, None), P())
    return jax.shard_map(shards, mesh=mesh, in_specs=in_specs, out_specs=out_specs, check_vma=False)
```

```python
import jax
import jax.numpy as jnp
from jax import lax
from jax.experimental import pallas as pl
from jax.experimental.pallas import tpu as pltpu
from jax.sharding import PartitionSpec as P

highest = lax.Precision.HIGHEST
f32 = jnp.float32
bf16 = jnp.bfloat16

R = 96
S = 4
W = S * R
VMEM = pl.BlockSpec(memory_space=pltpu.VMEM)


def dot(a, b, dims, precision=highest):
    return lax.dot_general(a, b, (dims, ((), ())), precision=precision, preferred_element_type=f32)


def lanes(shape):
    return lax.broadcasted_iota(jnp.int32, shape, 1)


def rows(shape):
    return lax.broadcasted_iota(jnp.int32, shape, 0)


def call(body, out, cost=None, scratch=()):
    shapes = [jax.ShapeDtypeStruct(o, f32) for o in out]

    def run(*args):
        return pl.pallas_call(
            body,
            out_shape=shapes,
            in_specs=[VMEM] * len(args),
            out_specs=[VMEM] * len(shapes),
            scratch_shapes=list(scratch),
            compiler_params=pltpu.CompilerParams(vmem_limit_bytes=32 * 1024 * 1024),
            cost_estimate=cost,
        )(*args)

    return run


def prepare(fb_ref, fc_ref, out_ref, z_ref):
    nc = fc_ref.shape[0]
    parts, depth = out_ref.shape[0], z_ref.shape[0] // out_ref.shape[0]
    low = lanes((R, 128)) <= rows((R, 128))
    flat = []
    for s in range(S):
        b = fb_ref[:, s, :]
        c = fc_ref[:, s, :]
        flat.append(c)
        wide_b = jnp.concatenate([b, jnp.zeros((b.shape[0], 128 - R), f32)], axis=1)
        wide_c = jnp.concatenate([c, jnp.zeros((c.shape[0], 128 - R), f32)], axis=1)
        gram_b = dot(b, wide_b, ((0,), (0,)))
        gram_c = dot(c, pltpu.roll(wide_c, 1, 1), ((0,), (0,)))
        z_ref[s * R : (s + 1) * R, :] = jnp.where(low, gram_b, gram_c)
    c_flat = jnp.concatenate(flat, axis=1)
    third = depth // 3
    for p in range(parts):
        out_ref[p, 0:nc, :] = c_flat
        for q in range(3):
            at = p * depth + q * third
            out_ref[p, nc : nc + third, q * 128 : (q + 1) * 128] = z_ref[at : at + third, :]


def middle(got_ref, fb_ref, out_ref, z_ref):
    parts = out_ref.shape[0]
    nb = fb_ref.shape[0]
    peers, third = got_ref.shape[0], z_ref.shape[0] // 3
    nc = got_ref.shape[1] - third
    share = got_ref[0, nc:, :]
    for p in range(1, peers):
        share = share + got_ref[p, nc:, :]
    for q in range(3):
        z_ref[q * third : (q + 1) * third, :] = share[:, q * 128 : (q + 1) * 128]
    b_flat = jnp.concatenate([fb_ref[:, s, :] for s in range(S)], axis=1)
    depth = z_ref.shape[0] // parts
    step = depth // 3
    for p in range(parts):
        out_ref[p, 0:nb, :] = b_flat
        for q in range(3):
            at = p * depth + q * step
            out_ref[p, nb : nb + step, q * 128 : (q + 1) * 128] = z_ref[at : at + step, :]
        out_ref[p, nb + step :, :] = jnp.zeros((out_ref.shape[1] - nb - step, W), f32)


def contract(t_ref, c_got_ref, b_got_ref, out_ref, m_ref):
    ni, nj, nk = t_ref.shape
    nc = nk // c_got_ref.shape[0]
    nb = nj // b_got_ref.shape[0]
    c = jnp.concatenate([c_got_ref[p, 0:nc, :] for p in range(c_got_ref.shape[0])], axis=0)
    b = jnp.concatenate([b_got_ref[p, 0:nb, :] for p in range(b_got_ref.shape[0])], axis=0)
    c_high = c.astype(bf16)
    c_low = (c - c_high.astype(f32)).astype(bf16)
    twice = jnp.concatenate([c_high, c_high], axis=0)
    group = 8
    for at in range(0, ni, group):
        t = t_ref[at : at + group, :, :].reshape(group * nj, nk)
        t_high = t.astype(bf16)
        t_low = (t - t_high.astype(f32)).astype(bf16)
        both = jnp.concatenate([t_high, t_low], axis=1)
        value = dot(both, twice, ((1,), (0,)), None) + dot(t_high, c_low, ((1,), (0,)), None)
        value = value.reshape(group, nj, W) * b[None]
        m_ref[at : at + group, :] = jnp.sum(value, axis=1)
    share = b_got_ref[0, nb : nb + 8, :]
    for p in range(1, b_got_ref.shape[0]):
        share = share + b_got_ref[p, nb : nb + 8, :]
    step = 4
    z = jnp.concatenate([share[0:step, q * 128 : (q + 1) * 128] for q in range(3)], axis=0)
    for p in range(out_ref.shape[0]):
        out_ref[p, 0 : 3 * step, :] = z
    pad = jnp.zeros((ni, 128 - R), f32)
    for s in range(S):
        one = jnp.concatenate([m_ref[:, s * R : (s + 1) * R], pad], axis=1)
        out_ref[:, 3 * step + s, :] = one


def own_row(got_ref, out_ref):
    total = jnp.sum(got_ref[:, 12:16, :], axis=0)
    out_ref[...] = jnp.broadcast_to(total[None], out_ref.shape)


def wide(v):
    return jnp.broadcast_to(v, (8, 128))


def eliminate(blocks, scale, k, q, lane8, row8):
    own, m = divmod(k, 8)
    hit = (lane8 >= k) & (lane8 < k + q)
    mine = blocks[own]
    row = [wide(mine[m + p : m + p + 1]) for p in range(q)]
    cols = [wide(mine[:, k + j : k + j + 1]) for j in range(q)]
    a = {(p, j): wide(cols[j][m + p : m + p + 1]) for p in range(q) for j in range(p, q)}
    inv, u, unit = [], {}, []
    for p in range(q):
        inv.append(1.0 / a[p, p])
        unit.append(jnp.where(lane8 == k + p, 1.0, row[p]))
        scale = jnp.where(lane8 == k + p, inv[p], scale)
        for i in range(p + 1, q):
            u[i, p] = a[p, i] * inv[p]
            for j in range(i, q):
                a[i, j] = a[i, j] - u[i, p] * a[p, j]
        for i in range(p + 1, q):
            row[i] = jnp.where(lane8 == k + p, 0.0, row[i]) - u[i, p] * unit[p]
    steps = [None] * q
    for p in reversed(range(q)):
        step = jnp.where((lane8 > k + p) & hit, 0.0, unit[p]) * inv[p]
        for j in range(p + 1, q):
            step = step - u[j, p] * steps[j]
        steps[p] = step
    for i in range(own, len(blocks)):
        old = blocks[i]
        new = jnp.where(hit, 0.0, old)
        for p in range(q):
            new = new - wide(old[:, k + p : k + p + 1]) * steps[p]
        if i == own:
            new = jnp.where(row8 >= m + q, new, old)
            for p in range(1, q):
                new = jnp.where(row8 == m + p, row[p], new)
        blocks[i] = new
    return scale


def invert(got_ref, out_ref, z_ref):
    for p in range(got_ref.shape[0]):
        z_ref[12 * p : 12 * (p + 1), :] = got_ref[p, 0:12, :]
    lane, row = lanes((R, 128)), rows((R, 128))
    fill = jnp.zeros((128 - R, 128), f32)
    blocks = []
    for s in range(S):
        z = z_ref[s * R : (s + 1) * R, :]
        low = jnp.where(lane <= row, z, 0.0)
        b_up = jnp.concatenate([low, fill], axis=0).T[0:R]
        c_up = pltpu.roll(z, 127, 1)
        up = jnp.where((lane >= row) & (lane < R), b_up * c_up, 0.0)
        strict = jnp.where(lane > row, up, 0.0)
        full = up + jnp.concatenate([strict, fill], axis=0).T[0:R]
        blocks.append([full[8 * i : 8 * i + 8] for i in range(R // 8)])
    lane8, row8 = lanes((8, 128)), rows((8, 1))
    scale = [jnp.zeros((8, 128), f32)] * S
    for k in range(0, R, 4):
        for s in range(S):
            scale[s] = eliminate(blocks[s], scale[s], k, 4, lane8, row8)
    for s in range(S):
        w = jnp.concatenate(blocks[s], axis=0)
        w = jnp.where(lane == row, 1.0, jnp.where(lane < row, w, 0.0))
        inv = jnp.sum(jnp.where(lane == row, scale[s][0:1], 0.0), axis=1, keepdims=True)
        out_ref[s] = dot(w[:, 0:R], w * inv, ((0,), (0,)))


def solve(m_ref, own_ref, inv_ref, out_ref, raw_ref):
    squares = []
    for s in range(S):
        inv = inv_ref[s]
        raw = dot(m_ref[:, s, 0:R], inv, ((1,), (0,)))
        squares.append(jnp.sum(raw * raw, axis=0, keepdims=True))
        raw_ref[s : s + 1, :] = dot(own_ref[0, :, 0:R], inv, ((1,), (0,)))[s : s + 1]
    total = jnp.concatenate(squares, axis=0)
    out_ref[...] = jnp.broadcast_to(total[None], out_ref.shape)


def finish_of(row_total):
    def finish(got_ref, raw_ref, fa_ref, w_ref):
        total = jnp.sum(got_ref[...], axis=0)
        weights = jnp.sqrt(total / row_total + 1e-06)
        w_ref[...] = weights[:, 0:R]
        fa_ref[0] = (raw_ref[...] / weights)[:, 0:R]

    return finish


def shards(tensor, factor_b, factor_c):
    ni = tensor.shape[0]
    ia, ja, ka = (lax.axis_size(a) for a in ("ia", "ja", "ka"))
    depth = S * R // ja
    grams = pltpu.VMEM((S * R, 128), f32)
    slots_c = call(prepare, [(ja, factor_c.shape[0] + depth // 3, W)], scratch=[grams])(factor_b, factor_c)[0]
    got_c = lax.all_to_all(slots_c, "ja", 0, 0)
    slots_b = call(middle, [(ka, factor_b.shape[0] + 8, W)], scratch=[pltpu.VMEM((depth, 128), f32)])(got_c, factor_b)[0]
    got_b = lax.all_to_all(slots_b, "ka", 0, 0)
    slots_m = call(contract, [(ja * ka, 16, 128)], scratch=[pltpu.VMEM((ni, W), f32)])(tensor, got_c, got_b)[0]
    got_m = lax.all_to_all(slots_m, ("ja", "ka"), 0, 0)
    own = call(own_row, [(ja * ka, S, 128)])(got_m)[0]
    all_rows = lax.all_to_all(own, ("ja", "ka"), 0, 0)
    cost = pl.CostEstimate(flops=int(1e10), bytes_accessed=int(4e7), transcendentals=0)
    inverse = call(invert, [(S, R, 128)], cost=cost, scratch=[grams])(got_m)[0]
    squares, raw = call(solve, [(ia, S, 128), (S, 128)])(all_rows, own, inverse)
    got_s = lax.all_to_all(squares, "ia", 0, 0)
    return tuple(call(finish_of(ni * ia), [(1, S, R), (S, R)])(got_s, raw))


def solution(mesh):
    in_specs = (P("ia", "ja", "ka"), P(("ja", "ka"), None, None), P(("ka", "ja"), None, None))
    out_specs = (P(("ia", "ja", "ka"), None, None), P())
    return jax.shard_map(shards, mesh=mesh, in_specs=in_specs, out_specs=out_specs, check_vma=False)
```

```python
import jax
import jax.numpy as jnp
from jax import lax
from jax.experimental import pallas as pl
from jax.experimental.pallas import tpu as pltpu
from jax.sharding import PartitionSpec as P

highest = lax.Precision.HIGHEST
f32 = jnp.float32
bf16 = jnp.bfloat16

R = 96
S = 4
W = S * R
VMEM = pl.BlockSpec(memory_space=pltpu.VMEM)


def dot(a, b, dims, precision=highest):
    return lax.dot_general(a, b, (dims, ((), ())), precision=precision, preferred_element_type=f32)


def lanes(shape):
    return lax.broadcasted_iota(jnp.int32, shape, 1)


def rows(shape):
    return lax.broadcasted_iota(jnp.int32, shape, 0)


def call(body, out, cost=None, scratch=()):
    shapes = [jax.ShapeDtypeStruct(o, f32) for o in out]

    def run(*args):
        return pl.pallas_call(
            body,
            out_shape=shapes,
            in_specs=[VMEM] * len(args),
            out_specs=[VMEM] * len(shapes),
            scratch_shapes=list(scratch),
            compiler_params=pltpu.CompilerParams(vmem_limit_bytes=32 * 1024 * 1024),
            cost_estimate=cost,
        )(*args)

    return run


def prepare(fb_ref, fc_ref, out_ref, z_ref):
    nc = fc_ref.shape[0]
    parts, depth = out_ref.shape[0], z_ref.shape[0] // out_ref.shape[0]
    low = lanes((R, 128)) <= rows((R, 128))
    flat = []
    for s in range(S):
        b = fb_ref[:, s, :]
        c = fc_ref[:, s, :]
        flat.append(c)
        wide_b = jnp.concatenate([b, jnp.zeros((b.shape[0], 128 - R), f32)], axis=1)
        wide_c = jnp.concatenate([c, jnp.zeros((c.shape[0], 128 - R), f32)], axis=1)
        gram_b = dot(b, wide_b, ((0,), (0,)))
        gram_c = dot(c, pltpu.roll(wide_c, 1, 1), ((0,), (0,)))
        z_ref[s * R : (s + 1) * R, :] = jnp.where(low, gram_b, gram_c)
    c_flat = jnp.concatenate(flat, axis=1)
    third = depth // 3
    for p in range(parts):
        out_ref[p, 0:nc, :] = c_flat
        for q in range(3):
            at = p * depth + q * third
            out_ref[p, nc : nc + third, q * 128 : (q + 1) * 128] = z_ref[at : at + third, :]


def middle(got_ref, fb_ref, out_ref):
    nb = fb_ref.shape[0]
    nc = got_ref.shape[1] - (out_ref.shape[1] - nb)
    share = jnp.sum(got_ref[:, nc:, :], axis=0)
    b_flat = jnp.concatenate([fb_ref[:, s, :] for s in range(S)], axis=1)
    for p in range(out_ref.shape[0]):
        out_ref[p, 0:nb, :] = b_flat
        out_ref[p, nb:, :] = share


def contract(t_ref, c_got_ref, b_got_ref, out_ref, m_ref):
    ni, nj, nk = t_ref.shape
    nc = nk // c_got_ref.shape[0]
    nb = nj // b_got_ref.shape[0]
    c = c_got_ref[:, 0:nc, :].reshape(nk, W)
    b = b_got_ref[:, 0:nb, :].reshape(nj, W)
    c_high = c.astype(bf16)
    c_low = (c - c_high.astype(f32)).astype(bf16)
    twice = jnp.concatenate([c_high, c_high], axis=0)
    group = 8
    for at in range(0, ni, group):
        t = t_ref[at : at + group, :, :].reshape(group * nj, nk)
        t_high = t.astype(bf16)
        t_low = (t - t_high.astype(f32)).astype(bf16)
        both = jnp.concatenate([t_high, t_low], axis=1)
        value = dot(both, twice, ((1,), (0,)), None) + dot(t_high, c_low, ((1,), (0,)), None)
        value = value.reshape(group, nj, W) * b[None]
        m_ref[at : at + group, :] = jnp.sum(value, axis=1)
    share = jnp.sum(b_got_ref[:, nb:, :], axis=0)
    depth = share.shape[0]
    each = ni // out_ref.shape[0]
    pad = jnp.zeros((out_ref.shape[1] - depth - each, W), f32)
    for p in range(out_ref.shape[0]):
        out_ref[p, 0:depth, :] = share
        out_ref[p, depth : depth + each, :] = m_ref[each * p : each * (p + 1), :]
        out_ref[p, depth + each :, :] = pad


def own_rows(got_ref, out_ref):
    each = out_ref.shape[1]
    depth = S * R // got_ref.shape[0] // 3
    total = jnp.sum(got_ref[:, depth : depth + each, :], axis=0)
    out_ref[...] = jnp.broadcast_to(total[None], out_ref.shape)


def wide(v):
    return jnp.broadcast_to(v, (8, 128))


def eliminate(blocks, scale, k, q, lane8, row8):
    own, m = divmod(k, 8)
    hit = (lane8 >= k) & (lane8 < k + q)
    mine = blocks[own]
    row = [wide(mine[m + p : m + p + 1]) for p in range(q)]
    cols = [wide(mine[:, k + j : k + j + 1]) for j in range(q)]
    a = {(p, j): wide(cols[j][m + p : m + p + 1]) for p in range(q) for j in range(p, q)}
    inv, u, unit = [], {}, []
    for p in range(q):
        inv.append(1.0 / a[p, p])
        unit.append(jnp.where(lane8 == k + p, 1.0, row[p]))
        scale = jnp.where(lane8 == k + p, inv[p], scale)
        for i in range(p + 1, q):
            u[i, p] = a[p, i] * inv[p]
            for j in range(i, q):
                a[i, j] = a[i, j] - u[i, p] * a[p, j]
        for i in range(p + 1, q):
            row[i] = jnp.where(lane8 == k + p, 0.0, row[i]) - u[i, p] * unit[p]
    steps = [None] * q
    for p in reversed(range(q)):
        step = jnp.where((lane8 > k + p) & hit, 0.0, unit[p]) * inv[p]
        for j in range(p + 1, q):
            step = step - u[j, p] * steps[j]
        steps[p] = step
    for i in range(own, len(blocks)):
        old = blocks[i]
        new = jnp.where(hit, 0.0, old)
        for p in range(q):
            new = new - wide(old[:, k + p : k + p + 1]) * steps[p]
        if i == own:
            new = jnp.where(row8 >= m + q, new, old)
            for p in range(1, q):
                new = jnp.where(row8 == m + p, row[p], new)
        blocks[i] = new
    return scale


def invert(got_ref, out_ref, z_ref):
    third = S * R // got_ref.shape[0] // 3
    for p in range(got_ref.shape[0]):
        for q in range(3):
            at = (3 * p + q) * third
            z_ref[at : at + third, :] = got_ref[p, 0:third, q * 128 : (q + 1) * 128]
    lane, row = lanes((R, 128)), rows((R, 128))
    fill = jnp.zeros((128 - R, 128), f32)
    blocks = []
    for s in range(S):
        z = z_ref[s * R : (s + 1) * R, :]
        low = jnp.where(lane <= row, z, 0.0)
        b_up = jnp.concatenate([low, fill], axis=0).T[0:R]
        c_up = pltpu.roll(z, 127, 1)
        up = jnp.where((lane >= row) & (lane < R), b_up * c_up, 0.0)
        strict = jnp.where(lane > row, up, 0.0)
        full = up + jnp.concatenate([strict, fill], axis=0).T[0:R]
        blocks.append([full[8 * i : 8 * i + 8] for i in range(R // 8)])
    lane8, row8 = lanes((8, 128)), rows((8, 1))
    scale = [jnp.zeros((8, 128), f32)] * S
    for k in range(0, R, 4):
        for s in range(S):
            scale[s] = eliminate(blocks[s], scale[s], k, 4, lane8, row8)
    for s in range(S):
        w = jnp.concatenate(blocks[s], axis=0)
        w = jnp.where(lane == row, 1.0, jnp.where(lane < row, w, 0.0))
        inv = jnp.sum(jnp.where(lane == row, scale[s][0:1], 0.0), axis=1, keepdims=True)
        out_ref[s] = dot(w[:, 0:R], w * inv, ((0,), (0,)))


def solve(got_ref, inv_ref, out_ref, raw_ref, m_ref):
    peers = got_ref.shape[0]
    each = got_ref.shape[1]
    ka = lax.axis_size("ka")
    count = m_ref.shape[0] - 8
    for p in range(peers // ka):
        m_ref[each * p : each * (p + 1), :] = jnp.sum(got_ref[ka * p : ka * (p + 1)], axis=0)
    mine = m_ref[pl.ds(lax.axis_index("ia") * each + lax.axis_index("ka"), 1), :]
    m_ref[count:, :] = jnp.broadcast_to(mine, (8, W))
    squares = []
    for s in range(S):
        raw = dot(m_ref[:, s * R : (s + 1) * R], inv_ref[s], ((1,), (0,)))
        squares.append(jnp.sum(raw[0:count] * raw[0:count], axis=0, keepdims=True))
        raw_ref[s : s + 1, :] = raw[count : count + 1]
    out_ref[...] = jnp.broadcast_to(jnp.concatenate(squares, axis=0)[None], out_ref.shape)


def finish_of(row_total):
    def finish(got_ref, raw_ref, fa_ref, w_ref):
        total = jnp.sum(got_ref[...], axis=0)
        weights = jnp.sqrt(total / row_total + 1e-06)
        w_ref[...] = weights[:, 0:R]
        fa_ref[0] = (raw_ref[...] / weights)[:, 0:R]

    return finish


def shards(tensor, factor_b, factor_c):
    ni = tensor.shape[0]
    ia, ja, ka = (lax.axis_size(a) for a in ("ia", "ja", "ka"))
    nb, nc = factor_b.shape[0], factor_c.shape[0]
    third = S * R // ja // 3
    each = ni // ja
    grams = pltpu.VMEM((S * R, 128), f32)
    slots_c = call(prepare, [(ja, nc + third, W)], scratch=[grams])(factor_b, factor_c)[0]
    got_c = lax.all_to_all(slots_c, "ja", 0, 0)
    slots_b = call(middle, [(ka, nb + third, W)])(got_c, factor_b)[0]
    got_b = lax.all_to_all(slots_b, "ka", 0, 0)
    slots_m = call(contract, [(ja, third + 8, W)], scratch=[pltpu.VMEM((ni, W), f32)])(tensor, got_c, got_b)[0]
    got_m = lax.all_to_all(slots_m, "ja", 0, 0)
    own = call(own_rows, [(ia * ka, each, W)])(got_m)[0]
    got_t = lax.all_to_all(own, ("ia", "ka"), 0, 0)
    cost = pl.CostEstimate(flops=int(1e10), bytes_accessed=int(4e7), transcendentals=0)
    inverse = call(invert, [(S, R, 128)], cost=cost, scratch=[grams])(got_m)[0]
    squares, raw = call(solve, [(ja, S, 128), (S, 128)], scratch=[pltpu.VMEM((ia * each + 8, W), f32)])(got_t, inverse)
    got_s = lax.all_to_all(squares, "ja", 0, 0)
    return tuple(call(finish_of(ni * ia), [(1, S, R), (S, R)])(got_s, raw))


def solution(mesh):
    in_specs = (P("ia", "ja", "ka"), P(("ja", "ka"), None, None), P(("ka", "ja"), None, None))
    out_specs = (P(("ia", "ja", "ka"), None, None), P())
    return jax.shard_map(shards, mesh=mesh, in_specs=in_specs, out_specs=out_specs, check_vma=False)
```

```python
import jax
import jax.numpy as jnp
from jax import lax
from jax.experimental import pallas as pl
from jax.experimental.pallas import tpu as pltpu
from jax.sharding import PartitionSpec as P

highest = lax.Precision.HIGHEST
f32 = jnp.float32
bf16 = jnp.bfloat16

R = 96
S = 4
W = S * R
VMEM = pl.BlockSpec(memory_space=pltpu.VMEM)
HBM = pl.BlockSpec(memory_space=pltpu.HBM)


def dot(a, b, dims, precision=highest):
    return lax.dot_general(a, b, (dims, ((), ())), precision=precision, preferred_element_type=f32)


def lanes(shape):
    return lax.broadcasted_iota(jnp.int32, shape, 1)


def rows(shape):
    return lax.broadcasted_iota(jnp.int32, shape, 0)


def call(body, out, cost=None, scratch=(), hbm=0, limit=32):
    shapes = [jax.ShapeDtypeStruct(o, f32) for o in out]

    def run(*args):
        return pl.pallas_call(
            body,
            out_shape=shapes,
            in_specs=[HBM] * hbm + [VMEM] * (len(args) - hbm),
            out_specs=[VMEM] * len(shapes),
            scratch_shapes=list(scratch),
            compiler_params=pltpu.CompilerParams(vmem_limit_bytes=limit * 1024 * 1024),
            cost_estimate=cost,
        )(*args)

    return run


def prepare(fb_hbm, fc_hbm, out_ref, b_ref, z_ref, fb_ref, fc_ref, sems):
    copy_c = pltpu.make_async_copy(fc_hbm, fc_ref, sems.at[0])
    copy_b = pltpu.make_async_copy(fb_hbm, fb_ref, sems.at[1])
    copy_c.start()
    copy_b.start()
    copy_c.wait()
    parts, nc = out_ref.shape[0], fc_ref.shape[0]
    third = S * R // parts // 3
    c_flat = jnp.concatenate([fc_ref[:, s, :] for s in range(S)], axis=1)
    for p in range(parts):
        out_ref[p, 0:nc, :] = c_flat
    copy_b.wait()
    b_ref[...] = jnp.concatenate([fb_ref[:, s, :] for s in range(S)], axis=1)
    low = lanes((R, 128)) <= rows((R, 128))
    for s in range(S):
        b = fb_ref[:, s, :]
        c = fc_ref[:, s, :]
        wide_b = jnp.concatenate([b, jnp.zeros((b.shape[0], 128 - R), f32)], axis=1)
        wide_c = jnp.concatenate([c, jnp.zeros((c.shape[0], 128 - R), f32)], axis=1)
        gram_b = dot(b, wide_b, ((0,), (0,)))
        gram_c = dot(c, pltpu.roll(wide_c, 1, 1), ((0,), (0,)))
        z_ref[s * R : (s + 1) * R, :] = jnp.where(low, gram_b, gram_c)
    for p in range(parts):
        for q in range(3):
            at = (3 * p + q) * third
            out_ref[p, nc : nc + third, q * 128 : (q + 1) * 128] = z_ref[at : at + third, :]


def contract(t_hbm, c_got_ref, b_ref, out_ref, t_ref, m_ref, z_ref, sems):
    ni, nj, nk = t_ref.shape
    steps = sems.shape[0]
    group = ni // steps
    parts = [pl.ds(n * group, group) for n in range(steps)]
    copies = [pltpu.make_async_copy(t_hbm.at[p], t_ref.at[p], sems.at[n]) for n, p in enumerate(parts)]
    copies[0].start()
    copies[1].start()
    nc = nk // c_got_ref.shape[0]
    share = jnp.sum(c_got_ref[:, nc:, :], axis=0)
    third = share.shape[0]
    for q in range(3):
        z_ref[third * q : third * (q + 1), :] = share[:, q * 128 : (q + 1) * 128]
    for p in range(ni):
        at = 12 * (p % (third // 4))
        out_ref[p, 0:12, :] = z_ref[at : at + 12, :]
    out_ref[:, 15, :] = jnp.zeros((ni, 128), f32)
    c = c_got_ref[:, 0:nc, :].reshape(nk, W)
    b = b_ref[...]
    c_high = c.astype(bf16)
    c_low = (c - c_high.astype(f32)).astype(bf16)
    twice = jnp.concatenate([c_high, c_high], axis=0)
    for n in range(steps):
        copies[n].wait()
        if n + 2 < steps:
            copies[n + 2].start()
        at = n * group
        t = t_ref[at : at + group, :, :].reshape(group * nj, nk)
        t_high = t.astype(bf16)
        t_low = (t - t_high.astype(f32)).astype(bf16)
        both = jnp.concatenate([t_high, t_low], axis=1)
        value = dot(both, twice, ((1,), (0,)), None) + dot(t_high, c_low, ((1,), (0,)), None)
        m_ref[at : at + group, :] = jnp.sum(value.reshape(group, nj, W) * b[None], axis=1)
    for q in range(3):
        out_ref[:, 12 + q, :] = m_ref[:, q * 128 : (q + 1) * 128]


def total(got_ref, out_ref):
    ka = lax.axis_size("ka")
    share = jnp.sum(got_ref[pl.ds(lax.axis_index("ja") * ka, ka), 0:12, :], axis=0)
    out_ref[:, 0:12, :] = jnp.broadcast_to(share[None], (out_ref.shape[0], 12, 128))
    out_ref[:, 12:16, :] = jnp.broadcast_to(jnp.sum(got_ref[:, 12:16, :], axis=0)[None], (out_ref.shape[0], 4, 128))


def wide(v):
    return jnp.broadcast_to(v, (8, 128))


def eliminate(blocks, scale, k, q, lane8, row8):
    own, m = divmod(k, 8)
    hit = (lane8 >= k) & (lane8 < k + q)
    mine = blocks[own]
    row = [wide(mine[m + p : m + p + 1]) for p in range(q)]
    cols = [wide(mine[:, k + j : k + j + 1]) for j in range(q)]
    a = {(p, j): wide(cols[j][m + p : m + p + 1]) for p in range(q) for j in range(p, q)}
    inv, u, unit = [], {}, []
    for p in range(q):
        inv.append(1.0 / a[p, p])
        unit.append(jnp.where(lane8 == k + p, 1.0, row[p]))
        scale = jnp.where(lane8 == k + p, inv[p], scale)
        for i in range(p + 1, q):
            u[i, p] = a[p, i] * inv[p]
            for j in range(i, q):
                a[i, j] = a[i, j] - u[i, p] * a[p, j]
        for i in range(p + 1, q):
            row[i] = jnp.where(lane8 == k + p, 0.0, row[i]) - u[i, p] * unit[p]
    steps = [None] * q
    for p in reversed(range(q)):
        step = jnp.where((lane8 > k + p) & hit, 0.0, unit[p]) * inv[p]
        for j in range(p + 1, q):
            step = step - u[j, p] * steps[j]
        steps[p] = step
    for i in range(own, len(blocks)):
        old = blocks[i]
        new = jnp.where(hit, 0.0, old)
        for p in range(q):
            new = new - wide(old[:, k + p : k + p + 1]) * steps[p]
        if i == own:
            new = jnp.where(row8 >= m + q, new, old)
            for p in range(1, q):
                new = jnp.where(row8 == m + p, row[p], new)
        blocks[i] = new
    return scale


def solve(got_ref, own_ref, out_ref, raw_ref, z_ref, m_ref):
    count = got_ref.shape[0]
    for p in range(count):
        z_ref[12 * p : 12 * (p + 1), :] = got_ref[p, 0:12, :]
    for q in range(3):
        at = slice(q * 128, (q + 1) * 128)
        m_ref[0:count, at] = got_ref[:, 12 + q, :]
        m_ref[count:, at] = jnp.broadcast_to(own_ref[0, 12 + q : 13 + q, :], (m_ref.shape[0] - count, 128))
    lane, row = lanes((R, 128)), rows((R, 128))
    fill = jnp.zeros((128 - R, 128), f32)
    blocks = []
    for s in range(S):
        z = z_ref[s * R : (s + 1) * R, :]
        low = jnp.where(lane <= row, z, 0.0)
        b_up = jnp.concatenate([low, fill], axis=0).T[0:R]
        c_up = pltpu.roll(z, 127, 1)
        up = jnp.where((lane >= row) & (lane < R), b_up * c_up, 0.0)
        strict = jnp.where(lane > row, up, 0.0)
        full = up + jnp.concatenate([strict, fill], axis=0).T[0:R]
        blocks.append([full[8 * i : 8 * i + 8] for i in range(R // 8)])
    lane8, row8 = lanes((8, 128)), rows((8, 1))
    scale = [jnp.zeros((8, 128), f32)] * S
    for k in range(0, R, 4):
        for s in range(S):
            scale[s] = eliminate(blocks[s], scale[s], k, 4, lane8, row8)
    squares = []
    for s in range(S):
        w = jnp.concatenate(blocks[s], axis=0)
        w = jnp.where(lane == row, 1.0, jnp.where(lane < row, w, 0.0))
        half = dot(m_ref[:, s * R : (s + 1) * R], w[:, 0:R], ((1,), (1,))) * scale[s][0:1, 0:R]
        raw = dot(half, w, ((1,), (0,)))
        squares.append(jnp.sum(raw[0:count] * raw[0:count], axis=0, keepdims=True))
        raw_ref[s : s + 1, :] = raw[count : count + 1]
    out_ref[...] = jnp.broadcast_to(jnp.concatenate(squares, axis=0)[None], out_ref.shape)


def finish_of(row_total):
    def finish(got_ref, raw_ref, fa_ref, w_ref):
        total = jnp.sum(got_ref[...], axis=0)
        weights = jnp.sqrt(total / row_total + 1e-06)
        w_ref[...] = weights[:, 0:R]
        fa_ref[0] = (raw_ref[...] / weights)[:, 0:R]

    return finish


def shards(tensor, factor_b, factor_c):
    ni = tensor.shape[0]
    ia, ja, ka = (lax.axis_size(a) for a in ("ia", "ja", "ka"))
    nb, nc = factor_b.shape[0], factor_c.shape[0]
    third = S * R // ja // 3
    grams = pltpu.VMEM((S * R, 128), f32)
    slots_c, b_flat = call(
        prepare,
        [(ja, nc + third, W), (nb, W)],
        scratch=[grams, pltpu.VMEM(factor_b.shape, f32), pltpu.VMEM(factor_c.shape, f32), pltpu.SemaphoreType.DMA((2,))],
        hbm=2,
        limit=56,
    )(factor_b, factor_c)
    got_c = lax.all_to_all(slots_c, "ja", 0, 0)
    b_block = lax.all_gather(b_flat, "ka", axis=0, tiled=True)
    slots_m = call(
        contract,
        [(ja * ka, 16, 128)],
        scratch=[pltpu.VMEM(v, f32) for v in (tensor.shape, (ni, W), (3 * third, 128))] + [pltpu.SemaphoreType.DMA((8,))],
        hbm=1,
        limit=52,
    )(tensor, got_c, b_block)[0]
    got_m = lax.all_to_all(slots_m, ("ja", "ka"), 0, 0)
    own = call(total, [(ja * ka, 16, 128)])(got_m)[0]
    got_all = lax.all_to_all(own, ("ja", "ka"), 0, 0)
    squares, raw = call(solve, [(ia, S, 128), (S, 128)], scratch=[grams, pltpu.VMEM((ni + 8, W), f32)])(got_all, own)
    got_s = lax.all_to_all(squares, "ia", 0, 0)
    return tuple(call(finish_of(ni * ia), [(1, S, R), (S, R)])(got_s, raw))


def solution(mesh):
    in_specs = (P("ia", "ja", "ka"), P(("ja", "ka"), None, None), P(("ka", "ja"), None, None))
    out_specs = (P(("ia", "ja", "ka"), None, None), P())
    return jax.shard_map(shards, mesh=mesh, in_specs=in_specs, out_specs=out_specs, check_vma=False)
```

```python
import jax
import jax.numpy as jnp
from jax import lax
from jax.experimental import pallas as pl
from jax.experimental.pallas import tpu as pltpu
from jax.sharding import PartitionSpec as P

highest = lax.Precision.HIGHEST
f32 = jnp.float32
bf16 = jnp.bfloat16

R = 96
S = 4
W = S * R
VMEM = pl.BlockSpec(memory_space=pltpu.VMEM)
HBM = pl.BlockSpec(memory_space=pltpu.HBM)


def dot(a, b, dims, precision=highest):
    return lax.dot_general(a, b, (dims, ((), ())), precision=precision, preferred_element_type=f32)


def lanes(shape):
    return lax.broadcasted_iota(jnp.int32, shape, 1)


def rows(shape):
    return lax.broadcasted_iota(jnp.int32, shape, 0)


def call(body, out, cost=None, scratch=(), hbm=0, limit=32):
    shapes = [jax.ShapeDtypeStruct(o, f32) for o in out]

    def run(*args):
        return pl.pallas_call(
            body,
            out_shape=shapes,
            in_specs=[HBM] * hbm + [VMEM] * (len(args) - hbm),
            out_specs=[VMEM] * len(shapes),
            scratch_shapes=list(scratch),
            compiler_params=pltpu.CompilerParams(vmem_limit_bytes=limit * 1024 * 1024),
            cost_estimate=cost,
        )(*args)

    return run


def prepare(fb_hbm, fc_hbm, out_ref, b_ref, z_ref, fb_ref, fc_ref, sems):
    copy_c = pltpu.make_async_copy(fc_hbm, fc_ref, sems.at[0])
    copy_b = pltpu.make_async_copy(fb_hbm, fb_ref, sems.at[1])
    copy_c.start()
    copy_b.start()
    copy_c.wait()
    parts, nc = out_ref.shape[0], fc_ref.shape[0]
    third = S * R // parts // 3
    c_flat = jnp.concatenate([fc_ref[:, s, :] for s in range(S)], axis=1)
    for p in range(parts):
        out_ref[p, 0:nc, :] = c_flat
    copy_b.wait()
    b_ref[...] = jnp.concatenate([fb_ref[:, s, :] for s in range(S)], axis=1)
    low = lanes((R, 128)) <= rows((R, 128))
    for s in range(S):
        b = fb_ref[:, s, :]
        c = fc_ref[:, s, :]
        wide_b = jnp.concatenate([b, jnp.zeros((b.shape[0], 128 - R), f32)], axis=1)
        wide_c = jnp.concatenate([c, jnp.zeros((c.shape[0], 128 - R), f32)], axis=1)
        gram_b = dot(b, wide_b, ((0,), (0,)))
        gram_c = dot(c, pltpu.roll(wide_c, 1, 1), ((0,), (0,)))
        z_ref[s * R : (s + 1) * R, :] = jnp.where(low, gram_b, gram_c)
    for p in range(parts):
        for q in range(3):
            at = (3 * p + q) * third
            out_ref[p, nc : nc + third, q * 128 : (q + 1) * 128] = z_ref[at : at + third, :]


def middle(got_ref, out_ref):
    depth = out_ref.shape[1]
    share = jnp.sum(got_ref[:, got_ref.shape[1] - depth :, :], axis=0)
    out_ref[...] = jnp.broadcast_to(share[None], out_ref.shape)


def contract(t_ref, c_got_ref, b_ref, out_ref):
    ni, nj, nk = t_ref.shape
    c = c_got_ref[:, 0 : nk // c_got_ref.shape[0], :].reshape(nk, W)
    b = b_ref[...]
    c_high = c.astype(bf16)
    c_low = (c - c_high.astype(f32)).astype(bf16)
    twice = jnp.concatenate([c_high, c_high], axis=0)
    group = 8
    for at in range(0, ni, group):
        t = t_ref[at : at + group, :, :].reshape(group * nj, nk)
        t_high = t.astype(bf16)
        t_low = (t - t_high.astype(f32)).astype(bf16)
        both = jnp.concatenate([t_high, t_low], axis=1)
        value = dot(both, twice, ((1,), (0,)), None) + dot(t_high, c_low, ((1,), (0,)), None)
        out_ref[at : at + group, :] = jnp.sum(value.reshape(group, nj, W) * b[None], axis=1)


def pack(m_ref, z_got_ref, out_ref):
    share = jnp.sum(z_got_ref[...], axis=0)
    depth = share.shape[0]
    each = m_ref.shape[0] // out_ref.shape[0]
    pad = jnp.zeros((out_ref.shape[1] - depth - each, W), f32)
    for p in range(out_ref.shape[0]):
        out_ref[p, 0:depth, :] = share
        out_ref[p, depth : depth + each, :] = m_ref[each * p : each * (p + 1), :]
        out_ref[p, depth + each :, :] = pad


def rows_of(first):
    def sum_rows(got_ref, out_ref):
        each = out_ref.shape[1]
        out_ref[...] = jnp.broadcast_to(jnp.sum(got_ref[:, first : first + each, :], axis=0)[None], out_ref.shape)

    return sum_rows


def wide(v):
    return jnp.broadcast_to(v, (8, 128))


def eliminate(blocks, scale, k, q, lane8, row8):
    own, m = divmod(k, 8)
    hit = (lane8 >= k) & (lane8 < k + q)
    mine = blocks[own]
    row = [wide(mine[m + p : m + p + 1]) for p in range(q)]
    cols = [wide(mine[:, k + j : k + j + 1]) for j in range(q)]
    a = {(p, j): wide(cols[j][m + p : m + p + 1]) for p in range(q) for j in range(p, q)}
    inv, u, unit = [], {}, []
    for p in range(q):
        inv.append(1.0 / a[p, p])
        unit.append(jnp.where(lane8 == k + p, 1.0, row[p]))
        scale = jnp.where(lane8 == k + p, inv[p], scale)
        for i in range(p + 1, q):
            u[i, p] = a[p, i] * inv[p]
            for j in range(i, q):
                a[i, j] = a[i, j] - u[i, p] * a[p, j]
        for i in range(p + 1, q):
            row[i] = jnp.where(lane8 == k + p, 0.0, row[i]) - u[i, p] * unit[p]
    steps = [None] * q
    for p in reversed(range(q)):
        step = jnp.where((lane8 > k + p) & hit, 0.0, unit[p]) * inv[p]
        for j in range(p + 1, q):
            step = step - u[j, p] * steps[j]
        steps[p] = step
    for i in range(own, len(blocks)):
        old = blocks[i]
        new = jnp.where(hit, 0.0, old)
        for p in range(q):
            new = new - wide(old[:, k + p : k + p + 1]) * steps[p]
        if i == own:
            new = jnp.where(row8 >= m + q, new, old)
            for p in range(1, q):
                new = jnp.where(row8 == m + p, row[p], new)
        blocks[i] = new
    return scale


def invert(got_ref, out_ref, z_ref):
    third = S * R // got_ref.shape[0] // 3
    for p in range(got_ref.shape[0]):
        for q in range(3):
            at = (3 * p + q) * third
            z_ref[at : at + third, :] = got_ref[p, 0:third, q * 128 : (q + 1) * 128]
    lane, row = lanes((R, 128)), rows((R, 128))
    fill = jnp.zeros((128 - R, 128), f32)
    blocks = []
    for s in range(S):
        z = z_ref[s * R : (s + 1) * R, :]
        low = jnp.where(lane <= row, z, 0.0)
        b_up = jnp.concatenate([low, fill], axis=0).T[0:R]
        c_up = pltpu.roll(z, 127, 1)
        up = jnp.where((lane >= row) & (lane < R), b_up * c_up, 0.0)
        strict = jnp.where(lane > row, up, 0.0)
        full = up + jnp.concatenate([strict, fill], axis=0).T[0:R]
        blocks.append([full[8 * i : 8 * i + 8] for i in range(R // 8)])
    lane8, row8 = lanes((8, 128)), rows((8, 1))
    scale = [jnp.zeros((8, 128), f32)] * S
    for k in range(0, R, 4):
        for s in range(S):
            scale[s] = eliminate(blocks[s], scale[s], k, 4, lane8, row8)
    for s in range(S):
        w = jnp.concatenate(blocks[s], axis=0)
        w = jnp.where(lane == row, 1.0, jnp.where(lane < row, w, 0.0))
        inv = jnp.sum(jnp.where(lane == row, scale[s][0:1], 0.0), axis=1, keepdims=True)
        out_ref[s] = dot(w[:, 0:R], w * inv, ((0,), (0,)))


def solve(got_ref, own_ref, inv_ref, out_ref, raw_ref, m_ref):
    each = got_ref.shape[1]
    count = m_ref.shape[0] - 8
    for p in range(got_ref.shape[0]):
        m_ref[each * p : each * (p + 1), :] = got_ref[p]
    mine = own_ref[0, pl.ds(lax.axis_index("ka"), 1), :]
    m_ref[count:, :] = jnp.broadcast_to(mine, (8, W))
    squares = []
    for s in range(S):
        raw = dot(m_ref[:, s * R : (s + 1) * R], inv_ref[s], ((1,), (0,)))
        squares.append(jnp.sum(raw[0:count] * raw[0:count], axis=0, keepdims=True))
        raw_ref[s : s + 1, :] = raw[count : count + 1]
    out_ref[...] = jnp.broadcast_to(jnp.concatenate(squares, axis=0)[None], out_ref.shape)


def finish_of(row_total):
    def finish(got_ref, raw_ref, fa_ref, w_ref):
        total = jnp.sum(got_ref[...], axis=0)
        weights = jnp.sqrt(total / row_total + 1e-06)
        w_ref[...] = weights[:, 0:R]
        fa_ref[0] = (raw_ref[...] / weights)[:, 0:R]

    return finish


def work(flops, nbytes):
    return pl.CostEstimate(flops=int(flops), bytes_accessed=int(nbytes), transcendentals=0)


def shards(tensor, factor_b, factor_c):
    ni = tensor.shape[0]
    ia, ja, ka = (lax.axis_size(a) for a in ("ia", "ja", "ka"))
    nb, nc = factor_b.shape[0], factor_c.shape[0]
    third = S * R // ja // 3
    each = ni // ja
    grams = pltpu.VMEM((S * R, 128), f32)
    slots_c, b_flat = call(
        prepare,
        [(ja, nc + third, W), (nb, W)],
        scratch=[grams, pltpu.VMEM(factor_b.shape, f32), pltpu.VMEM(factor_c.shape, f32), pltpu.SemaphoreType.DMA((2,))],
        hbm=2,
        limit=56,
    )(factor_b, factor_c)
    got_c = lax.all_to_all(slots_c, "ja", 0, 0)
    b_block = lax.all_gather(b_flat, "ka", axis=0, tiled=True)
    got_z = lax.all_to_all(call(middle, [(ka, third, W)])(got_c)[0], "ka", 0, 0)
    m_part = call(contract, [(ni, W)], cost=work(2e9, 4e6))(tensor, got_c, b_block)[0]
    got_m = lax.all_to_all(call(pack, [(ja, third + 8, W)])(m_part, got_z)[0], "ja", 0, 0)
    got_k = lax.all_to_all(call(rows_of(third), [(ka, each, W)])(got_m)[0], "ka", 0, 0)
    own = call(rows_of(0), [(ja, each, W)])(got_k)[0]
    got_j = lax.all_to_all(own, "ja", 0, 0)
    inverse = call(invert, [(S, R, 128)], cost=work(1e10, 4e7), scratch=[grams])(got_m)[0]
    squares, raw = call(solve, [(ia, S, 128), (S, 128)], scratch=[pltpu.VMEM((ni + 8, W), f32)])(got_j, own, inverse)
    got_s = lax.all_to_all(squares, "ia", 0, 0)
    return tuple(call(finish_of(ni * ia), [(1, S, R), (S, R)])(got_s, raw))


def solution(mesh):
    in_specs = (P("ia", "ja", "ka"), P(("ja", "ka"), None, None), P(("ka", "ja"), None, None))
    out_specs = (P(("ia", "ja", "ka"), None, None), P())
    return jax.shard_map(shards, mesh=mesh, in_specs=in_specs, out_specs=out_specs, check_vma=False)
```

```python
import jax
import jax.numpy as jnp
from jax import lax
from jax.experimental import pallas as pl
from jax.experimental.pallas import tpu as pltpu
from jax.sharding import PartitionSpec as P

highest = lax.Precision.HIGHEST
f32 = jnp.float32
bf16 = jnp.bfloat16

R = 96
S = 4
HALF = 2
W = S * R
VMEM = pl.BlockSpec(memory_space=pltpu.VMEM)


def dot(a, b, dims, precision=highest):
    return lax.dot_general(a, b, (dims, ((), ())), precision=precision, preferred_element_type=f32)


def lanes(shape):
    return lax.broadcasted_iota(jnp.int32, shape, 1)


def rows(shape):
    return lax.broadcasted_iota(jnp.int32, shape, 0)


def call(body, out, cost=None, scratch=()):
    shapes = [jax.ShapeDtypeStruct(o, f32) for o in out]

    def run(*args):
        return pl.pallas_call(
            body,
            out_shape=shapes,
            in_specs=[VMEM] * len(args),
            out_specs=[VMEM] * len(shapes),
            scratch_shapes=list(scratch),
            compiler_params=pltpu.CompilerParams(vmem_limit_bytes=32 * 1024 * 1024),
            cost_estimate=cost,
        )(*args)

    return run


def half():
    return lax.rem(lax.axis_index("ia"), 2)


def prepare(fb_ref, fc_ref, out_ref, z_ref):
    nc = fc_ref.shape[0]
    parts, depth = out_ref.shape[0], HALF * R // out_ref.shape[0]
    low = lanes((R, 128)) <= rows((R, 128))
    flat = []
    for s in range(S):
        b = fb_ref[:, s, :]
        c = fc_ref[:, s, :]
        flat.append(c)
        wide_b = jnp.concatenate([b, jnp.zeros((b.shape[0], 128 - R), f32)], axis=1)
        wide_c = jnp.concatenate([c, jnp.zeros((c.shape[0], 128 - R), f32)], axis=1)
        gram_b = dot(b, wide_b, ((0,), (0,)))
        gram_c = dot(c, pltpu.roll(wide_c, 1, 1), ((0,), (0,)))
        z_ref[s * R : (s + 1) * R, :] = jnp.where(low, gram_b, gram_c)
    c_flat = jnp.concatenate(flat, axis=1)
    third = depth // 3
    for p in range(parts):
        out_ref[p, 0:nc, :] = c_flat
        for q in range(3):
            at = pl.multiple_of(half() * HALF * R + p * depth + q * third, 8)
            out_ref[p, nc : nc + third, q * 128 : (q + 1) * 128] = z_ref[pl.ds(at, third), :]


def middle(got_ref, fb_ref, out_ref, z_ref):
    parts = out_ref.shape[0]
    nb = fb_ref.shape[0]
    peers, third = got_ref.shape[0], z_ref.shape[0] // 3
    nc = got_ref.shape[1] - third
    share = got_ref[0, nc:, :]
    for p in range(1, peers):
        share = share + got_ref[p, nc:, :]
    for q in range(3):
        z_ref[q * third : (q + 1) * third, :] = share[:, q * 128 : (q + 1) * 128]
    b_flat = jnp.concatenate([fb_ref[:, s, :] for s in range(S)], axis=1)
    depth = z_ref.shape[0] // parts
    step = depth // 3
    for p in range(parts):
        out_ref[p, 0:nb, :] = b_flat
        for q in range(3):
            at = p * depth + q * step
            out_ref[p, nb : nb + step, q * 128 : (q + 1) * 128] = z_ref[at : at + step, :]
        out_ref[p, nb + step :, :] = jnp.zeros((out_ref.shape[1] - nb - step, W), f32)


def contract(t_ref, c_got_ref, b_got_ref, out_ref, m_ref):
    ni, nj, nk = t_ref.shape
    nc = nk // c_got_ref.shape[0]
    nb = nj // b_got_ref.shape[0]
    c = jnp.concatenate([c_got_ref[p, 0:nc, :] for p in range(c_got_ref.shape[0])], axis=0)
    b = jnp.concatenate([b_got_ref[p, 0:nb, :] for p in range(b_got_ref.shape[0])], axis=0)
    c_high = c.astype(bf16)
    c_low = (c - c_high.astype(f32)).astype(bf16)
    twice = jnp.concatenate([c_high, c_high], axis=0)
    group = 8
    for at in range(0, ni, group):
        t = t_ref[at : at + group, :, :].reshape(group * nj, nk)
        t_high = t.astype(bf16)
        t_low = (t - t_high.astype(f32)).astype(bf16)
        both = jnp.concatenate([t_high, t_low], axis=1)
        value = dot(both, twice, ((1,), (0,)), None) + dot(t_high, c_low, ((1,), (0,)), None)
        value = value.reshape(group, nj, W) * b[None]
        m_ref[at : at + group, :] = jnp.sum(value, axis=1)
    share = b_got_ref[0, nb : nb + 8, :]
    for p in range(1, b_got_ref.shape[0]):
        share = share + b_got_ref[p, nb : nb + 8, :]
    step = HALF
    z = jnp.concatenate([share[0:step, q * 128 : (q + 1) * 128] for q in range(3)], axis=0)
    for p in range(out_ref.shape[0]):
        out_ref[p, 0 : 3 * step, :] = z
        out_ref[p, 3 * step : 12, :] = jnp.zeros((12 - 3 * step, 128), f32)
    pad = jnp.zeros((ni, 128 - R), f32)
    for s in range(S):
        one = jnp.concatenate([m_ref[:, s * R : (s + 1) * R], pad], axis=1)
        out_ref[:, 12 + s, :] = one


def own_row(got_ref, out_ref):
    total = jnp.sum(got_ref[:, 12:16, :], axis=0)
    out_ref[...] = jnp.broadcast_to(total[None], out_ref.shape)


def wide(v):
    return jnp.broadcast_to(v, (8, 128))


def eliminate(blocks, scale, k, q, lane8, row8):
    own, m = divmod(k, 8)
    hit = (lane8 >= k) & (lane8 < k + q)
    mine = blocks[own]
    row = [wide(mine[m + p : m + p + 1]) for p in range(q)]
    cols = [wide(mine[:, k + j : k + j + 1]) for j in range(q)]
    a = {(p, j): wide(cols[j][m + p : m + p + 1]) for p in range(q) for j in range(p, q)}
    inv, u, unit = [], {}, []
    for p in range(q):
        inv.append(1.0 / a[p, p])
        unit.append(jnp.where(lane8 == k + p, 1.0, row[p]))
        scale = jnp.where(lane8 == k + p, inv[p], scale)
        for i in range(p + 1, q):
            u[i, p] = a[p, i] * inv[p]
            for j in range(i, q):
                a[i, j] = a[i, j] - u[i, p] * a[p, j]
        for i in range(p + 1, q):
            row[i] = jnp.where(lane8 == k + p, 0.0, row[i]) - u[i, p] * unit[p]
    steps = [None] * q
    for p in reversed(range(q)):
        step = jnp.where((lane8 > k + p) & hit, 0.0, unit[p]) * inv[p]
        for j in range(p + 1, q):
            step = step - u[j, p] * steps[j]
        steps[p] = step
    for i in range(own, len(blocks)):
        old = blocks[i]
        new = jnp.where(hit, 0.0, old)
        for p in range(q):
            new = new - wide(old[:, k + p : k + p + 1]) * steps[p]
        if i == own:
            new = jnp.where(row8 >= m + q, new, old)
            for p in range(1, q):
                new = jnp.where(row8 == m + p, row[p], new)
        blocks[i] = new
    return scale


def invert(got_ref, out_ref, z_ref):
    for p in range(got_ref.shape[0]):
        z_ref[6 * p : 6 * (p + 1), :] = got_ref[p, 0:6, :]
    lane, row = lanes((R, 128)), rows((R, 128))
    fill = jnp.zeros((128 - R, 128), f32)
    blocks = []
    for s in range(HALF):
        z = z_ref[s * R : (s + 1) * R, :]
        low = jnp.where(lane <= row, z, 0.0)
        b_up = jnp.concatenate([low, fill], axis=0).T[0:R]
        c_up = pltpu.roll(z, 127, 1)
        up = jnp.where((lane >= row) & (lane < R), b_up * c_up, 0.0)
        strict = jnp.where(lane > row, up, 0.0)
        full = up + jnp.concatenate([strict, fill], axis=0).T[0:R]
        blocks.append([full[8 * i : 8 * i + 8] for i in range(R // 8)])
    lane8, row8 = lanes((8, 128)), rows((8, 1))
    scale = [jnp.zeros((8, 128), f32)] * HALF
    for k in range(0, R, 4):
        for s in range(HALF):
            scale[s] = eliminate(blocks[s], scale[s], k, 4, lane8, row8)
    for s in range(HALF):
        w = jnp.concatenate(blocks[s], axis=0)
        w = jnp.where(lane == row, 1.0, jnp.where(lane < row, w, 0.0))
        inv = jnp.sum(jnp.where(lane == row, scale[s][0:1], 0.0), axis=1, keepdims=True)
        out_ref[s] = dot(w[:, 0:R], w * inv, ((0,), (0,)))


def solve(m_ref, own_ref, mine_ref, other_ref, out_ref, raw_ref):
    squares = []
    for s in range(S):
        inv = jnp.where(half() == s // HALF, mine_ref[s % HALF], other_ref[s % HALF])
        raw = dot(m_ref[:, s, 0:R], inv, ((1,), (0,)))
        squares.append(jnp.sum(raw * raw, axis=0, keepdims=True))
        raw_ref[s : s + 1, :] = dot(own_ref[0, :, 0:R], inv, ((1,), (0,)))[s : s + 1]
    total = jnp.concatenate(squares, axis=0)
    out_ref[...] = jnp.broadcast_to(total[None], out_ref.shape)


def finish_of(row_total):
    def finish(got_ref, raw_ref, fa_ref, w_ref):
        total = jnp.sum(got_ref[...], axis=0)
        weights = jnp.sqrt(total / row_total + 1e-06)
        w_ref[...] = weights[:, 0:R]
        fa_ref[0] = (raw_ref[...] / weights)[:, 0:R]

    return finish


def shards(tensor, factor_b, factor_c):
    ni = tensor.shape[0]
    ia, ja, ka = (lax.axis_size(a) for a in ("ia", "ja", "ka"))
    depth = HALF * R // ja
    cost = pl.CostEstimate(flops=int(1e10), bytes_accessed=int(4e7), transcendentals=0)
    grams = pltpu.VMEM((S * R, 128), f32)
    slots_c = call(prepare, [(ja, factor_c.shape[0] + depth // 3, W)], scratch=[grams])(factor_b, factor_c)[0]
    got_c = lax.all_to_all(slots_c, "ja", 0, 0)
    slots_b = call(middle, [(ka, factor_b.shape[0] + 8, W)], cost=cost, scratch=[pltpu.VMEM((depth, 128), f32)])(got_c, factor_b)[0]
    got_b = lax.all_to_all(slots_b, "ka", 0, 0)
    slots_m = call(contract, [(ja * ka, 16, 128)], scratch=[pltpu.VMEM((ni, W), f32)])(tensor, got_c, got_b)[0]
    got_m = lax.all_to_all(slots_m, ("ja", "ka"), 0, 0)
    own = call(own_row, [(ja * ka, S, 128)])(got_m)[0]
    all_rows = lax.all_to_all(own, ("ja", "ka"), 0, 0)
    inverse = call(invert, [(HALF, R, 128)], cost=cost, scratch=[grams])(got_m)[0]
    other = lax.ppermute(inverse, "ia", [(n, n ^ 1) for n in range(ia)])
    squares, raw = call(solve, [(ia, S, 128), (S, 128)])(all_rows, own, inverse, other)
    got_s = lax.all_to_all(squares, "ia", 0, 0)
    return tuple(call(finish_of(ni * ia), [(1, S, R), (S, R)])(got_s, raw))


def solution(mesh):
    in_specs = (P("ia", "ja", "ka"), P(("ja", "ka"), None, None), P(("ka", "ja"), None, None))
    out_specs = (P(("ia", "ja", "ka"), None, None), P())
    return jax.shard_map(shards, mesh=mesh, in_specs=in_specs, out_specs=out_specs, check_vma=False)
```

```python
import jax
import jax.numpy as jnp
from jax import lax
from jax.experimental import pallas as pl
from jax.experimental.pallas import tpu as pltpu
from jax.sharding import PartitionSpec as P

highest = lax.Precision.HIGHEST
f32 = jnp.float32
bf16 = jnp.bfloat16

R = 96
S = 4
W = S * R
VMEM = pl.BlockSpec(memory_space=pltpu.VMEM)


def dot(a, b, dims, precision=highest):
    return lax.dot_general(a, b, (dims, ((), ())), precision=precision, preferred_element_type=f32)


def lanes(shape):
    return lax.broadcasted_iota(jnp.int32, shape, 1)


def rows(shape):
    return lax.broadcasted_iota(jnp.int32, shape, 0)


def call(body, out, cost=None, scratch=()):
    shapes = [jax.ShapeDtypeStruct(o, f32) for o in out]

    def run(*args):
        return pl.pallas_call(
            body,
            out_shape=shapes,
            in_specs=[VMEM] * len(args),
            out_specs=[VMEM] * len(shapes),
            scratch_shapes=list(scratch),
            compiler_params=pltpu.CompilerParams(vmem_limit_bytes=32 * 1024 * 1024),
            cost_estimate=cost,
        )(*args)

    return run


def start_of():
    return lax.rem(lax.axis_index("ia"), S)


def pick(which, choices):
    out = choices[0]
    for n in range(1, len(choices)):
        out = jnp.where(which == n, choices[n], out)
    return out


def prepare(fb_ref, fc_ref, out_ref):
    peers, nc = out_ref.shape[0], fc_ref.shape[0]
    b = pick(start_of(), [fb_ref[:, s, :] for s in range(S)])
    c = pick(start_of(), [fc_ref[:, s, :] for s in range(S)])
    wide_b = jnp.concatenate([b, jnp.zeros((b.shape[0], 128 - R), f32)], axis=1)
    wide_c = jnp.concatenate([c, jnp.zeros((c.shape[0], 128 - R), f32)], axis=1)
    gram_b = dot(b, wide_b, ((0,), (0,)))
    gram_c = dot(c, pltpu.roll(wide_c, 1, 1), ((0,), (0,)))
    z = jnp.where(lanes((R, 128)) <= rows((R, 128)), gram_b, gram_c)
    c_flat = jnp.concatenate([fc_ref[:, s, :] for s in range(S)], axis=1)
    depth = R // peers
    fill = jnp.zeros((out_ref.shape[1] - 3 * nc - depth, 128), f32)
    for p in range(peers):
        for q in range(3):
            out_ref[p, q * nc : (q + 1) * nc, :] = c_flat[:, q * 128 : (q + 1) * 128]
        out_ref[p, 3 * nc :, :] = jnp.concatenate([z[p * depth : (p + 1) * depth], fill], axis=0)


def middle(got_ref, fb_ref, out_ref):
    parts, nb = out_ref.shape[0], fb_ref.shape[0]
    depth = R // got_ref.shape[0]
    share = jnp.sum(got_ref[:, got_ref.shape[1] - 16 :, :], axis=0)
    b_flat = jnp.concatenate([fb_ref[:, s, :] for s in range(S)], axis=1)
    step = depth // parts
    fill = jnp.zeros((8 - step, 128), f32)
    for p in range(parts):
        for q in range(3):
            out_ref[p, q * nb : (q + 1) * nb, :] = b_flat[:, q * 128 : (q + 1) * 128]
        out_ref[p, 3 * nb :, :] = jnp.concatenate([share[p * step : (p + 1) * step], fill], axis=0)


def gathered(ref, count):
    pieces = [ref[:, q * count : (q + 1) * count, :].reshape(ref.shape[0] * count, 128) for q in range(3)]
    return jnp.concatenate(pieces, axis=1)


def contract(t_ref, c_got_ref, b_got_ref, out_ref, m_ref):
    ni, nj, nk = t_ref.shape
    nb = nj // b_got_ref.shape[0]
    c = gathered(c_got_ref, nk // c_got_ref.shape[0])
    b = gathered(b_got_ref, nb)
    c_high = c.astype(bf16)
    c_low = (c - c_high.astype(f32)).astype(bf16)
    twice = jnp.concatenate([c_high, c_high], axis=0)
    group = 8
    for at in range(0, ni, group):
        t = t_ref[at : at + group, :, :].reshape(group * nj, nk)
        t_high = t.astype(bf16)
        t_low = (t - t_high.astype(f32)).astype(bf16)
        both = jnp.concatenate([t_high, t_low], axis=1)
        value = dot(both, twice, ((1,), (0,)), None) + dot(t_high, c_low, ((1,), (0,)), None)
        m_ref[at : at + group, :] = jnp.sum(value.reshape(group, nj, W) * b[None], axis=1)
    share = jnp.sum(b_got_ref[:, 3 * nb :, :], axis=0)
    out_ref[...] = jnp.broadcast_to(share[None], out_ref.shape)
    for q in range(3):
        out_ref[:, 3 + q, :] = m_ref[:, q * 128 : (q + 1) * 128]


def own_row(got_ref, out_ref):
    total = jnp.sum(got_ref[...], axis=0)
    flat = jnp.concatenate([total[3 + q : 4 + q] for q in range(3)], axis=1)
    pad = jnp.zeros((1, 128 - R), f32)
    row = [jnp.concatenate([flat[:, s * R : (s + 1) * R], pad], axis=1) for s in range(S)]
    out_ref[...] = jnp.broadcast_to(jnp.concatenate(row, axis=0)[None], out_ref.shape)


def wide(v):
    return jnp.broadcast_to(v, (8, 128))


def eliminate(blocks, scale, k, q, lane8, row8):
    own, m = divmod(k, 8)
    hit = (lane8 >= k) & (lane8 < k + q)
    mine = blocks[own]
    row = [wide(mine[m + p : m + p + 1]) for p in range(q)]
    cols = [wide(mine[:, k + j : k + j + 1]) for j in range(q)]
    a = {(p, j): wide(cols[j][m + p : m + p + 1]) for p in range(q) for j in range(p, q)}
    inv, u, unit = [], {}, []
    for p in range(q):
        inv.append(1.0 / a[p, p])
        unit.append(jnp.where(lane8 == k + p, 1.0, row[p]))
        scale = jnp.where(lane8 == k + p, inv[p], scale)
        for i in range(p + 1, q):
            u[i, p] = a[p, i] * inv[p]
            for j in range(i, q):
                a[i, j] = a[i, j] - u[i, p] * a[p, j]
        for i in range(p + 1, q):
            row[i] = jnp.where(lane8 == k + p, 0.0, row[i]) - u[i, p] * unit[p]
    steps = [None] * q
    for p in reversed(range(q)):
        step = jnp.where((lane8 > k + p) & hit, 0.0, unit[p]) * inv[p]
        for j in range(p + 1, q):
            step = step - u[j, p] * steps[j]
        steps[p] = step
    for i in range(own, len(blocks)):
        old = blocks[i]
        new = jnp.where(hit, 0.0, old)
        for p in range(q):
            new = new - wide(old[:, k + p : k + p + 1]) * steps[p]
        if i == own:
            new = jnp.where(row8 >= m + q, new, old)
            for p in range(1, q):
                new = jnp.where(row8 == m + p, row[p], new)
        blocks[i] = new
    return scale


def invert(got_ref, out_ref, z_ref):
    for p in range(got_ref.shape[0]):
        z_ref[3 * p : 3 * (p + 1), :] = got_ref[p, 0:3, :]
    lane, row = lanes((R, 128)), rows((R, 128))
    fill = jnp.zeros((128 - R, 128), f32)
    blocks = []
    for s in range(1):
        z = z_ref[s * R : (s + 1) * R, :]
        low = jnp.where(lane <= row, z, 0.0)
        b_up = jnp.concatenate([low, fill], axis=0).T[0:R]
        c_up = pltpu.roll(z, 127, 1)
        up = jnp.where((lane >= row) & (lane < R), b_up * c_up, 0.0)
        strict = jnp.where(lane > row, up, 0.0)
        full = up + jnp.concatenate([strict, fill], axis=0).T[0:R]
        blocks.append([full[8 * i : 8 * i + 8] for i in range(R // 8)])
    lane8, row8 = lanes((8, 128)), rows((8, 1))
    scale = [jnp.zeros((8, 128), f32)]
    for k in range(0, R, 4):
        for s in range(1):
            scale[s] = eliminate(blocks[s], scale[s], k, 4, lane8, row8)
    for s in range(1):
        w = jnp.concatenate(blocks[s], axis=0)
        w = jnp.where(lane == row, 1.0, jnp.where(lane < row, w, 0.0))
        inv = jnp.sum(jnp.where(lane == row, scale[s][0:1], 0.0), axis=1, keepdims=True)
        out_ref[s] = dot(w[:, 0:R], w * inv, ((0,), (0,)))


def solve(m_ref, own_ref, *refs):
    inverses, (out_ref, raw_ref) = [ref[0] for ref in refs[:S]], refs[S:]
    squares = []
    for s in range(S):
        inv = pick(start_of() ^ s, inverses)
        raw = dot(m_ref[:, s, 0:R], inv, ((1,), (0,)))
        squares.append(jnp.sum(raw * raw, axis=0, keepdims=True))
        raw_ref[s : s + 1, :] = dot(own_ref[0, :, 0:R], inv, ((1,), (0,)))[s : s + 1]
    total = jnp.concatenate(squares, axis=0)
    out_ref[...] = jnp.broadcast_to(total[None], out_ref.shape)


def finish_of(row_total):
    def finish(got_ref, raw_ref, fa_ref, w_ref):
        total = jnp.sum(got_ref[...], axis=0)
        weights = jnp.sqrt(total / row_total + 1e-06)
        w_ref[...] = weights[:, 0:R]
        fa_ref[0] = (raw_ref[...] / weights)[:, 0:R]

    return finish


def shards(tensor, factor_b, factor_c):
    ni = tensor.shape[0]
    ia, ja, ka = (lax.axis_size(a) for a in ("ia", "ja", "ka"))
    nb, nc = factor_b.shape[0], factor_c.shape[0]
    cost = pl.CostEstimate(flops=int(1e10), bytes_accessed=int(4e7), transcendentals=0)
    slots_c = call(prepare, [(ja, 3 * nc + 16, 128)])(factor_b, factor_c)[0]
    got_c = lax.all_to_all(slots_c, "ja", 0, 0)
    slots_b = call(middle, [(ka, 3 * nb + 8, 128)], cost=cost)(got_c, factor_b)[0]
    got_b = lax.all_to_all(slots_b, "ka", 0, 0)
    slots_m = call(contract, [(ja * ka, 8, 128)], scratch=[pltpu.VMEM((ni, W), f32)])(tensor, got_c, got_b)[0]
    got_m = lax.all_to_all(slots_m, ("ja", "ka"), 0, 0)
    own = call(own_row, [(ja * ka, S, 128)])(got_m)[0]
    all_rows = lax.all_to_all(own, ("ja", "ka"), 0, 0)
    inverse = call(invert, [(1, R, 128)], cost=cost, scratch=[pltpu.VMEM((R, 128), f32)])(got_m)[0]
    others = [lax.ppermute(inverse, "ia", [(n, n ^ d) for n in range(ia)]) for d in range(1, S)]
    squares, raw = call(solve, [(ia, S, 128), (S, 128)])(all_rows, own, inverse, *others)
    got_s = lax.all_to_all(squares, "ia", 0, 0)
    return tuple(call(finish_of(ni * ia), [(1, S, R), (S, R)])(got_s, raw))


def solution(mesh):
    in_specs = (P("ia", "ja", "ka"), P(("ja", "ka"), None, None), P(("ka", "ja"), None, None))
    out_specs = (P(("ia", "ja", "ka"), None, None), P())
    return jax.shard_map(shards, mesh=mesh, in_specs=in_specs, out_specs=out_specs, check_vma=False)
```

```python
import jax
import jax.numpy as jnp
from jax import lax
from jax.experimental import pallas as pl
from jax.experimental.pallas import tpu as pltpu
from jax.sharding import PartitionSpec as P

highest = lax.Precision.HIGHEST
f32 = jnp.float32
bf16 = jnp.bfloat16

R = 96
S = 4
W = S * R
VMEM = pl.BlockSpec(memory_space=pltpu.VMEM)


def dot(a, b, dims, precision=highest):
    return lax.dot_general(a, b, (dims, ((), ())), precision=precision, preferred_element_type=f32)


def lanes(shape):
    return lax.broadcasted_iota(jnp.int32, shape, 1)


def rows(shape):
    return lax.broadcasted_iota(jnp.int32, shape, 0)


def call(body, out, cost=None, scratch=()):
    shapes = [jax.ShapeDtypeStruct(o, f32) for o in out]

    def run(*args):
        return pl.pallas_call(
            body,
            out_shape=shapes,
            in_specs=[VMEM] * len(args),
            out_specs=[VMEM] * len(shapes),
            scratch_shapes=list(scratch),
            compiler_params=pltpu.CompilerParams(vmem_limit_bytes=32 * 1024 * 1024),
            cost_estimate=cost,
        )(*args)

    return run


def start_of():
    return lax.rem(lax.axis_index("ia"), S)


def pick(which, choices):
    out = choices[0]
    for n in range(1, len(choices)):
        out = jnp.where(which == n, choices[n], out)
    return out


def prepare(fb_ref, fc_ref, out_ref):
    peers, nc = out_ref.shape[0], fc_ref.shape[0]
    b = pick(start_of(), [fb_ref[:, s, :] for s in range(S)])
    c = pick(start_of(), [fc_ref[:, s, :] for s in range(S)])
    wide_b = jnp.concatenate([b, jnp.zeros((b.shape[0], 128 - R), f32)], axis=1)
    wide_c = jnp.concatenate([c, jnp.zeros((c.shape[0], 128 - R), f32)], axis=1)
    gram_b = dot(b, wide_b, ((0,), (0,)))
    gram_c = dot(c, pltpu.roll(wide_c, 1, 1), ((0,), (0,)))
    z = jnp.where(lanes((R, 128)) <= rows((R, 128)), gram_b, gram_c)
    c_flat = jnp.concatenate([fc_ref[:, s, :] for s in range(S)], axis=1)
    depth = R // peers
    fill = jnp.zeros((out_ref.shape[1] - 3 * nc - depth, 128), f32)
    for p in range(peers):
        for q in range(3):
            out_ref[p, q * nc : (q + 1) * nc, :] = c_flat[:, q * 128 : (q + 1) * 128]
        out_ref[p, 3 * nc :, :] = jnp.concatenate([z[p * depth : (p + 1) * depth], fill], axis=0)


def middle(got_ref, fb_ref, out_ref):
    parts, nb = out_ref.shape[0], fb_ref.shape[0]
    depth = R // got_ref.shape[0]
    share = jnp.sum(got_ref[:, got_ref.shape[1] - 16 :, :], axis=0)
    b_flat = jnp.concatenate([fb_ref[:, s, :] for s in range(S)], axis=1)
    step = depth // parts
    fill = jnp.zeros((8 - step, 128), f32)
    for p in range(parts):
        for q in range(3):
            out_ref[p, q * nb : (q + 1) * nb, :] = b_flat[:, q * 128 : (q + 1) * 128]
        out_ref[p, 3 * nb :, :] = jnp.concatenate([share[p * step : (p + 1) * step], fill], axis=0)


def gathered(ref, count):
    pieces = [ref[:, q * count : (q + 1) * count, :].reshape(ref.shape[0] * count, 128) for q in range(3)]
    return jnp.concatenate(pieces, axis=1)


def contract(t_ref, c_got_ref, b_got_ref, out_ref, m_ref):
    ni, nj, nk = t_ref.shape
    nb = nj // b_got_ref.shape[0]
    c = gathered(c_got_ref, nk // c_got_ref.shape[0])
    b = gathered(b_got_ref, nb)
    c_high = c.astype(bf16)
    c_low = (c - c_high.astype(f32)).astype(bf16)
    twice = jnp.concatenate([c_high, c_high], axis=0)
    group = 8
    for at in range(0, ni, group):
        t = t_ref[at : at + group, :, :].reshape(group * nj, nk)
        t_high = t.astype(bf16)
        t_low = (t - t_high.astype(f32)).astype(bf16)
        both = jnp.concatenate([t_high, t_low], axis=1)
        value = dot(both, twice, ((1,), (0,)), None) + dot(t_high, c_low, ((1,), (0,)), None)
        m_ref[at : at + group, :] = jnp.sum(value.reshape(group, nj, W) * b[None], axis=1)
    share = jnp.sum(b_got_ref[:, 3 * nb :, :], axis=0)
    out_ref[...] = jnp.broadcast_to(share[None], out_ref.shape)
    for q in range(3):
        out_ref[:, 3 + q, :] = m_ref[:, q * 128 : (q + 1) * 128]


def own_row(got_ref, out_ref):
    total = jnp.sum(got_ref[...], axis=0)
    flat = jnp.concatenate([total[3 + q : 4 + q] for q in range(3)], axis=1)
    pad = jnp.zeros((1, 128 - R), f32)
    row = [jnp.concatenate([flat[:, s * R : (s + 1) * R], pad], axis=1) for s in range(S)]
    out_ref[...] = jnp.broadcast_to(jnp.concatenate(row, axis=0)[None], out_ref.shape)


def wide(v):
    return jnp.broadcast_to(v, (8, 128))


def eliminate(blocks, scale, k, q, lane8, row8):
    own, m = divmod(k, 8)
    hit = (lane8 >= k) & (lane8 < k + q)
    mine = blocks[own]
    row = [wide(mine[m + p : m + p + 1]) for p in range(q)]
    cols = [wide(mine[:, k + j : k + j + 1]) for j in range(q)]
    a = {(p, j): wide(cols[j][m + p : m + p + 1]) for p in range(q) for j in range(p, q)}
    inv, u, unit = [], {}, []
    for p in range(q):
        inv.append(1.0 / a[p, p])
        unit.append(jnp.where(lane8 == k + p, 1.0, row[p]))
        scale = jnp.where(lane8 == k + p, inv[p], scale)
        for i in range(p + 1, q):
            u[i, p] = a[p, i] * inv[p]
            for j in range(i, q):
                a[i, j] = a[i, j] - u[i, p] * a[p, j]
        for i in range(p + 1, q):
            row[i] = jnp.where(lane8 == k + p, 0.0, row[i]) - u[i, p] * unit[p]
    steps = [None] * q
    for p in reversed(range(q)):
        step = jnp.where((lane8 > k + p) & hit, 0.0, unit[p]) * inv[p]
        for j in range(p + 1, q):
            step = step - u[j, p] * steps[j]
        steps[p] = step
    for i in range(own, len(blocks)):
        old = blocks[i]
        new = jnp.where(hit, 0.0, old)
        for p in range(q):
            new = new - wide(old[:, k + p : k + p + 1]) * steps[p]
        if i == own:
            new = jnp.where(row8 >= m + q, new, old)
            for p in range(1, q):
                new = jnp.where(row8 == m + p, row[p], new)
        blocks[i] = new
    return scale


def invert(got_ref, out_ref, z_ref):
    for p in range(got_ref.shape[0]):
        z_ref[3 * p : 3 * (p + 1), :] = got_ref[p, 0:3, :]
    lane, row = lanes((R, 128)), rows((R, 128))
    fill = jnp.zeros((128 - R, 128), f32)
    blocks = []
    for s in range(1):
        z = z_ref[s * R : (s + 1) * R, :]
        low = jnp.where(lane <= row, z, 0.0)
        b_up = jnp.concatenate([low, fill], axis=0).T[0:R]
        c_up = pltpu.roll(z, 127, 1)
        up = jnp.where((lane >= row) & (lane < R), b_up * c_up, 0.0)
        strict = jnp.where(lane > row, up, 0.0)
        full = up + jnp.concatenate([strict, fill], axis=0).T[0:R]
        blocks.append([full[8 * i : 8 * i + 8] for i in range(R // 8)])
    lane8, row8 = lanes((8, 128)), rows((8, 1))
    scale = [jnp.zeros((8, 128), f32)]
    for k in range(0, R, 8):
        for s in range(1):
            scale[s] = eliminate(blocks[s], scale[s], k, 8, lane8, row8)
    for s in range(1):
        w = jnp.concatenate(blocks[s], axis=0)
        w = jnp.where(lane == row, 1.0, jnp.where(lane < row, w, 0.0))
        inv = jnp.sum(jnp.where(lane == row, scale[s][0:1], 0.0), axis=1, keepdims=True)
        out_ref[s] = dot(w[:, 0:R], w * inv, ((0,), (0,)))


def solve(m_ref, own_ref, *refs):
    inverses, (out_ref, raw_ref) = [ref[0] for ref in refs[:S]], refs[S:]
    count = m_ref.shape[0]
    squares = []
    for s in range(S):
        inv = pick(start_of() ^ s, inverses)
        both = jnp.concatenate([m_ref[:, s, 0:R], own_ref[0:8, s, 0:R]], axis=0)
        raw = dot(both, inv, ((1,), (0,)))
        squares.append(jnp.sum(raw[0:count] * raw[0:count], axis=0, keepdims=True))
        raw_ref[s : s + 1, :] = raw[count : count + 1]
    total = jnp.concatenate(squares, axis=0)
    out_ref[...] = jnp.broadcast_to(total[None], out_ref.shape)


def finish_of(row_total):
    def finish(got_ref, raw_ref, fa_ref, w_ref):
        total = jnp.sum(got_ref[...], axis=0)
        weights = jnp.sqrt(total / row_total + 1e-06)
        w_ref[...] = weights[:, 0:R]
        fa_ref[0] = (raw_ref[...] / weights)[:, 0:R]

    return finish


def shards(tensor, factor_b, factor_c):
    ni = tensor.shape[0]
    ia, ja, ka = (lax.axis_size(a) for a in ("ia", "ja", "ka"))
    nb, nc = factor_b.shape[0], factor_c.shape[0]
    cost = pl.CostEstimate(flops=int(1e10), bytes_accessed=int(4e7), transcendentals=0)
    slots_c = call(prepare, [(ja, 3 * nc + 16, 128)])(factor_b, factor_c)[0]
    got_c = lax.all_to_all(slots_c, "ja", 0, 0)
    slots_b = call(middle, [(ka, 3 * nb + 8, 128)], cost=cost)(got_c, factor_b)[0]
    got_b = lax.all_to_all(slots_b, "ka", 0, 0)
    slots_m = call(contract, [(ja * ka, 8, 128)], scratch=[pltpu.VMEM((ni, W), f32)])(tensor, got_c, got_b)[0]
    got_m = lax.all_to_all(slots_m, ("ja", "ka"), 0, 0)
    own = call(own_row, [(ja * ka, S, 128)])(got_m)[0]
    all_rows = lax.all_to_all(own, ("ja", "ka"), 0, 0)
    inverse = call(invert, [(1, R, 128)], cost=cost, scratch=[pltpu.VMEM((R, 128), f32)])(got_m)[0]
    others = [lax.ppermute(inverse, "ia", [(n, n ^ d) for n in range(ia)]) for d in range(1, S)]
    squares, raw = call(solve, [(ia, S, 128), (S, 128)])(all_rows, own, inverse, *others)
    got_s = lax.all_to_all(squares, "ia", 0, 0)
    return tuple(call(finish_of(ni * ia), [(1, S, R), (S, R)])(got_s, raw))


def solution(mesh):
    in_specs = (P("ia", "ja", "ka"), P(("ja", "ka"), None, None), P(("ka", "ja"), None, None))
    out_specs = (P(("ia", "ja", "ka"), None, None), P())
    return jax.shard_map(shards, mesh=mesh, in_specs=in_specs, out_specs=out_specs, check_vma=False)
```

```python
import jax
import jax.numpy as jnp
from jax import lax
from jax.experimental import pallas as pl
from jax.experimental.pallas import tpu as pltpu
from jax.sharding import PartitionSpec as P

highest = lax.Precision.HIGHEST
f32 = jnp.float32
bf16 = jnp.bfloat16

R = 96
S = 4
W = S * R
VMEM = pl.BlockSpec(memory_space=pltpu.VMEM)


def dot(a, b, dims, precision=highest):
    return lax.dot_general(a, b, (dims, ((), ())), precision=precision, preferred_element_type=f32)


def lanes(shape):
    return lax.broadcasted_iota(jnp.int32, shape, 1)


def rows(shape):
    return lax.broadcasted_iota(jnp.int32, shape, 0)


def call(body, out, cost=None, scratch=()):
    shapes = [jax.ShapeDtypeStruct(o, f32) for o in out]

    def run(*args):
        return pl.pallas_call(
            body,
            out_shape=shapes,
            in_specs=[VMEM] * len(args),
            out_specs=[VMEM] * len(shapes),
            scratch_shapes=list(scratch),
            compiler_params=pltpu.CompilerParams(vmem_limit_bytes=32 * 1024 * 1024),
            cost_estimate=cost,
        )(*args)

    return run


def start_of():
    return lax.rem(lax.axis_index("ia"), S)


def pick(which, choices):
    out = choices[0]
    for n in range(1, len(choices)):
        out = jnp.where(which == n, choices[n], out)
    return out


def prepare(fb_ref, fc_ref, out_ref, b_ref):
    peers, nc = out_ref.shape[0], fc_ref.shape[0]
    b = pick(start_of(), [fb_ref[:, s, :] for s in range(S)])
    c = pick(start_of(), [fc_ref[:, s, :] for s in range(S)])
    wide_b = jnp.concatenate([b, jnp.zeros((b.shape[0], 128 - R), f32)], axis=1)
    wide_c = jnp.concatenate([c, jnp.zeros((c.shape[0], 128 - R), f32)], axis=1)
    gram_b = dot(b, wide_b, ((0,), (0,)))
    gram_c = dot(c, pltpu.roll(wide_c, 1, 1), ((0,), (0,)))
    z = jnp.where(lanes((R, 128)) <= rows((R, 128)), gram_b, gram_c)
    c_flat = jnp.concatenate([fc_ref[:, s, :] for s in range(S)], axis=1)
    b_ref[...] = jnp.concatenate([fb_ref[:, s, :] for s in range(S)], axis=1)
    depth = R // peers
    fill = jnp.zeros((out_ref.shape[1] - 3 * nc - depth, 128), f32)
    for p in range(peers):
        for q in range(3):
            out_ref[p, q * nc : (q + 1) * nc, :] = c_flat[:, q * 128 : (q + 1) * 128]
        out_ref[p, 3 * nc :, :] = jnp.concatenate([z[p * depth : (p + 1) * depth], fill], axis=0)


def gathered(ref, count):
    pieces = [ref[:, q * count : (q + 1) * count, :].reshape(ref.shape[0] * count, 128) for q in range(3)]
    return jnp.concatenate(pieces, axis=1)


def contract(t_ref, c_got_ref, b_ref, out_ref, m_ref):
    ni, nj, nk = t_ref.shape
    nc = nk // c_got_ref.shape[0]
    c = gathered(c_got_ref, nc)
    b = b_ref[...]
    c_high = c.astype(bf16)
    c_low = (c - c_high.astype(f32)).astype(bf16)
    twice = jnp.concatenate([c_high, c_high], axis=0)
    group = 8
    for at in range(0, ni, group):
        t = t_ref[at : at + group, :, :].reshape(group * nj, nk)
        t_high = t.astype(bf16)
        t_low = (t - t_high.astype(f32)).astype(bf16)
        both = jnp.concatenate([t_high, t_low], axis=1)
        value = dot(both, twice, ((1,), (0,)), None) + dot(t_high, c_low, ((1,), (0,)), None)
        m_ref[at : at + group, :] = jnp.sum(value.reshape(group, nj, W) * b[None], axis=1)
    share = jnp.sum(c_got_ref[:, 3 * nc :, :], axis=0)
    out_ref[...] = jnp.broadcast_to(share[None], out_ref.shape)
    for q in range(3):
        out_ref[:, 12 + q, :] = m_ref[:, q * 128 : (q + 1) * 128]


def own_row(got_ref, out_ref):
    total = jnp.sum(got_ref[:, 8:16, :], axis=0)
    flat = jnp.concatenate([total[4 + q : 5 + q] for q in range(3)], axis=1)
    pad = jnp.zeros((1, 128 - R), f32)
    row = [jnp.concatenate([flat[:, s * R : (s + 1) * R], pad], axis=1) for s in range(S)]
    out_ref[...] = jnp.broadcast_to(jnp.concatenate(row, axis=0)[None], out_ref.shape)


def wide(v):
    return jnp.broadcast_to(v, (8, 128))


def eliminate(blocks, scale, k, q, lane8, row8):
    own, m = divmod(k, 8)
    hit = (lane8 >= k) & (lane8 < k + q)
    mine = blocks[own]
    row = [wide(mine[m + p : m + p + 1]) for p in range(q)]
    cols = [wide(mine[:, k + j : k + j + 1]) for j in range(q)]
    a = {(p, j): wide(cols[j][m + p : m + p + 1]) for p in range(q) for j in range(p, q)}
    inv, u, unit = [], {}, []
    for p in range(q):
        inv.append(1.0 / a[p, p])
        unit.append(jnp.where(lane8 == k + p, 1.0, row[p]))
        scale = jnp.where(lane8 == k + p, inv[p], scale)
        for i in range(p + 1, q):
            u[i, p] = a[p, i] * inv[p]
            for j in range(i, q):
                a[i, j] = a[i, j] - u[i, p] * a[p, j]
        for i in range(p + 1, q):
            row[i] = jnp.where(lane8 == k + p, 0.0, row[i]) - u[i, p] * unit[p]
    steps = [None] * q
    for p in reversed(range(q)):
        step = jnp.where((lane8 > k + p) & hit, 0.0, unit[p]) * inv[p]
        for j in range(p + 1, q):
            step = step - u[j, p] * steps[j]
        steps[p] = step
    for i in range(own, len(blocks)):
        old = blocks[i]
        new = jnp.where(hit, 0.0, old)
        for p in range(q):
            new = new - wide(old[:, k + p : k + p + 1]) * steps[p]
        if i == own:
            new = jnp.where(row8 >= m + q, new, old)
            for p in range(1, q):
                new = jnp.where(row8 == m + p, row[p], new)
        blocks[i] = new
    return scale


def invert(got_ref, out_ref, z_ref):
    ka = lax.axis_size("ka")
    for p in range(got_ref.shape[0] // ka):
        z_ref[12 * p : 12 * (p + 1), :] = jnp.sum(got_ref[ka * p : ka * (p + 1), 0:12, :], axis=0)
    lane, row = lanes((R, 128)), rows((R, 128))
    fill = jnp.zeros((128 - R, 128), f32)
    blocks = []
    for s in range(1):
        z = z_ref[s * R : (s + 1) * R, :]
        low = jnp.where(lane <= row, z, 0.0)
        b_up = jnp.concatenate([low, fill], axis=0).T[0:R]
        c_up = pltpu.roll(z, 127, 1)
        up = jnp.where((lane >= row) & (lane < R), b_up * c_up, 0.0)
        strict = jnp.where(lane > row, up, 0.0)
        full = up + jnp.concatenate([strict, fill], axis=0).T[0:R]
        blocks.append([full[8 * i : 8 * i + 8] for i in range(R // 8)])
    lane8, row8 = lanes((8, 128)), rows((8, 1))
    scale = [jnp.zeros((8, 128), f32)]
    for k in range(0, R, 8):
        for s in range(1):
            scale[s] = eliminate(blocks[s], scale[s], k, 8, lane8, row8)
    for s in range(1):
        w = jnp.concatenate(blocks[s], axis=0)
        w = jnp.where(lane == row, 1.0, jnp.where(lane < row, w, 0.0))
        inv = jnp.sum(jnp.where(lane == row, scale[s][0:1], 0.0), axis=1, keepdims=True)
        out_ref[s] = dot(w[:, 0:R], w * inv, ((0,), (0,)))


def solve(m_ref, own_ref, *refs):
    inverses, (out_ref, raw_ref) = [ref[0] for ref in refs[:S]], refs[S:]
    count = m_ref.shape[0]
    squares = []
    for s in range(S):
        inv = pick(start_of() ^ s, inverses)
        both = jnp.concatenate([m_ref[:, s, 0:R], own_ref[0:8, s, 0:R]], axis=0)
        raw = dot(both, inv, ((1,), (0,)))
        squares.append(jnp.sum(raw[0:count] * raw[0:count], axis=0, keepdims=True))
        raw_ref[s : s + 1, :] = raw[count : count + 1]
    total = jnp.concatenate(squares, axis=0)
    out_ref[...] = jnp.broadcast_to(total[None], out_ref.shape)


def finish_of(row_total):
    def finish(got_ref, raw_ref, fa_ref, w_ref):
        total = jnp.sum(got_ref[...], axis=0)
        weights = jnp.sqrt(total / row_total + 1e-06)
        w_ref[...] = weights[:, 0:R]
        fa_ref[0] = (raw_ref[...] / weights)[:, 0:R]

    return finish


def shards(tensor, factor_b, factor_c):
    ni = tensor.shape[0]
    ia, ja, ka = (lax.axis_size(a) for a in ("ia", "ja", "ka"))
    nb, nc = factor_b.shape[0], factor_c.shape[0]
    cost = pl.CostEstimate(flops=int(1e10), bytes_accessed=int(4e7), transcendentals=0)
    slots_c, b_flat = call(prepare, [(ja, 3 * nc + 16, 128), (nb, W)], cost=cost)(factor_b, factor_c)
    got_c = lax.all_to_all(slots_c, "ja", 0, 0)
    b_block = lax.all_gather(b_flat, "ka", axis=0, tiled=True)
    slots_m = call(contract, [(ja * ka, 16, 128)], scratch=[pltpu.VMEM((ni, W), f32)])(tensor, got_c, b_block)[0]
    got_m = lax.all_to_all(slots_m, ("ja", "ka"), 0, 0)
    own = call(own_row, [(ja * ka, S, 128)])(got_m)[0]
    all_rows = lax.all_to_all(own, ("ja", "ka"), 0, 0)
    inverse = call(invert, [(1, R, 128)], cost=cost, scratch=[pltpu.VMEM((R, 128), f32)])(got_m)[0]
    others = [lax.ppermute(inverse, "ia", [(n, n ^ d) for n in range(ia)]) for d in range(1, S)]
    squares, raw = call(solve, [(ia, S, 128), (S, 128)])(all_rows, own, inverse, *others)
    got_s = lax.all_to_all(squares, "ia", 0, 0)
    return tuple(call(finish_of(ni * ia), [(1, S, R), (S, R)])(got_s, raw))


def solution(mesh):
    in_specs = (P("ia", "ja", "ka"), P(("ja", "ka"), None, None), P(("ka", "ja"), None, None))
    out_specs = (P(("ia", "ja", "ka"), None, None), P())
    return jax.shard_map(shards, mesh=mesh, in_specs=in_specs, out_specs=out_specs, check_vma=False)
```

```python
import jax
import jax.numpy as jnp
from jax import lax
from jax.experimental import pallas as pl
from jax.experimental.pallas import tpu as pltpu
from jax.sharding import PartitionSpec as P

highest = lax.Precision.HIGHEST
f32 = jnp.float32
bf16 = jnp.bfloat16

R = 96
S = 4
W = S * R
VMEM = pl.BlockSpec(memory_space=pltpu.VMEM)
HBM = pl.BlockSpec(memory_space=pltpu.HBM)


def dot(a, b, dims, precision=highest):
    return lax.dot_general(a, b, (dims, ((), ())), precision=precision, preferred_element_type=f32)


def lanes(shape):
    return lax.broadcasted_iota(jnp.int32, shape, 1)


def rows(shape):
    return lax.broadcasted_iota(jnp.int32, shape, 0)


def call(body, out, cost=None, scratch=(), hbm=0, limit=32):
    shapes = [jax.ShapeDtypeStruct(o, f32) for o in out]

    def run(*args):
        return pl.pallas_call(
            body,
            out_shape=shapes,
            in_specs=[HBM] * hbm + [VMEM] * (len(args) - hbm),
            out_specs=[VMEM] * len(shapes),
            scratch_shapes=list(scratch),
            compiler_params=pltpu.CompilerParams(vmem_limit_bytes=limit * 1024 * 1024),
            cost_estimate=cost,
        )(*args)

    return run


def start_of():
    return lax.rem(lax.axis_index("ia"), S)


def pick(which, choices):
    out = choices[0]
    for n in range(1, len(choices)):
        out = jnp.where(which == n, choices[n], out)
    return out


def prepare(fb_hbm, fc_hbm, out_ref, b_ref, fb_ref, fc_ref, sems):
    copy_b = pltpu.make_async_copy(fb_hbm, fb_ref, sems.at[0])
    copy_c = pltpu.make_async_copy(fc_hbm, fc_ref, sems.at[1])
    copy_b.start()
    copy_c.start()
    copy_b.wait()
    copy_c.wait()
    peers, nc = out_ref.shape[0], fc_ref.shape[0]
    b = pick(start_of(), [fb_ref[:, s, :] for s in range(S)])
    c = pick(start_of(), [fc_ref[:, s, :] for s in range(S)])
    wide_b = jnp.concatenate([b, jnp.zeros((b.shape[0], 128 - R), f32)], axis=1)
    wide_c = jnp.concatenate([c, jnp.zeros((c.shape[0], 128 - R), f32)], axis=1)
    gram_b = dot(b, wide_b, ((0,), (0,)))
    gram_c = dot(c, pltpu.roll(wide_c, 1, 1), ((0,), (0,)))
    z = jnp.where(lanes((R, 128)) <= rows((R, 128)), gram_b, gram_c)
    c_flat = jnp.concatenate([fc_ref[:, s, :] for s in range(S)], axis=1)
    b_ref[...] = jnp.concatenate([fb_ref[:, s, :] for s in range(S)], axis=1)
    depth = R // peers
    fill = jnp.zeros((out_ref.shape[1] - 3 * nc - depth, 128), f32)
    for p in range(peers):
        for q in range(3):
            out_ref[p, q * nc : (q + 1) * nc, :] = c_flat[:, q * 128 : (q + 1) * 128]
        out_ref[p, 3 * nc :, :] = jnp.concatenate([z[p * depth : (p + 1) * depth], fill], axis=0)


def gathered(ref, count):
    pieces = [ref[:, q * count : (q + 1) * count, :].reshape(ref.shape[0] * count, 128) for q in range(3)]
    return jnp.concatenate(pieces, axis=1)


def contract(t_ref, c_got_ref, b_ref, out_ref, m_ref):
    ni, nj, nk = t_ref.shape
    nc = nk // c_got_ref.shape[0]
    c = gathered(c_got_ref, nc)
    b = b_ref[...]
    c_high = c.astype(bf16)
    c_low = (c - c_high.astype(f32)).astype(bf16)
    twice = jnp.concatenate([c_high, c_high], axis=0)
    group = 8
    for at in range(0, ni, group):
        t = t_ref[at : at + group, :, :].reshape(group * nj, nk)
        t_high = t.astype(bf16)
        t_low = (t - t_high.astype(f32)).astype(bf16)
        both = jnp.concatenate([t_high, t_low], axis=1)
        value = dot(both, twice, ((1,), (0,)), None) + dot(t_high, c_low, ((1,), (0,)), None)
        m_ref[at : at + group, :] = jnp.sum(value.reshape(group, nj, W) * b[None], axis=1)
    share = jnp.sum(c_got_ref[:, 3 * nc :, :], axis=0)
    out_ref[...] = jnp.broadcast_to(share[None], out_ref.shape)
    for q in range(3):
        out_ref[:, 12 + q, :] = m_ref[:, q * 128 : (q + 1) * 128]


def own_row(got_ref, out_ref):
    total = jnp.sum(got_ref[:, 8:16, :], axis=0)
    flat = jnp.concatenate([total[4 + q : 5 + q] for q in range(3)], axis=1)
    pad = jnp.zeros((1, 128 - R), f32)
    row = [jnp.concatenate([flat[:, s * R : (s + 1) * R], pad], axis=1) for s in range(S)]
    out_ref[...] = jnp.broadcast_to(jnp.concatenate(row, axis=0)[None], out_ref.shape)


def wide(v):
    return jnp.broadcast_to(v, (8, 128))


def eliminate(blocks, scale, k, q, lane8, row8):
    own, m = divmod(k, 8)
    hit = (lane8 >= k) & (lane8 < k + q)
    mine = blocks[own]
    row = [wide(mine[m + p : m + p + 1]) for p in range(q)]
    cols = [wide(mine[:, k + j : k + j + 1]) for j in range(q)]
    a = {(p, j): wide(cols[j][m + p : m + p + 1]) for p in range(q) for j in range(p, q)}
    inv, u, unit = [], {}, []
    for p in range(q):
        inv.append(1.0 / a[p, p])
        unit.append(jnp.where(lane8 == k + p, 1.0, row[p]))
        scale = jnp.where(lane8 == k + p, inv[p], scale)
        for i in range(p + 1, q):
            u[i, p] = a[p, i] * inv[p]
            for j in range(i, q):
                a[i, j] = a[i, j] - u[i, p] * a[p, j]
        for i in range(p + 1, q):
            row[i] = jnp.where(lane8 == k + p, 0.0, row[i]) - u[i, p] * unit[p]
    steps = [None] * q
    for p in reversed(range(q)):
        step = jnp.where((lane8 > k + p) & hit, 0.0, unit[p]) * inv[p]
        for j in range(p + 1, q):
            step = step - u[j, p] * steps[j]
        steps[p] = step
    for i in range(own, len(blocks)):
        old = blocks[i]
        new = jnp.where(hit, 0.0, old)
        for p in range(q):
            new = new - wide(old[:, k + p : k + p + 1]) * steps[p]
        if i == own:
            new = jnp.where(row8 >= m + q, new, old)
            for p in range(1, q):
                new = jnp.where(row8 == m + p, row[p], new)
        blocks[i] = new
    return scale


def invert(got_ref, out_ref, z_ref):
    ka = lax.axis_size("ka")
    for p in range(got_ref.shape[0] // ka):
        z_ref[12 * p : 12 * (p + 1), :] = jnp.sum(got_ref[ka * p : ka * (p + 1), 0:12, :], axis=0)
    lane, row = lanes((R, 128)), rows((R, 128))
    fill = jnp.zeros((128 - R, 128), f32)
    blocks = []
    for s in range(1):
        z = z_ref[s * R : (s + 1) * R, :]
        low = jnp.where(lane <= row, z, 0.0)
        b_up = jnp.concatenate([low, fill], axis=0).T[0:R]
        c_up = pltpu.roll(z, 127, 1)
        up = jnp.where((lane >= row) & (lane < R), b_up * c_up, 0.0)
        strict = jnp.where(lane > row, up, 0.0)
        full = up + jnp.concatenate([strict, fill], axis=0).T[0:R]
        blocks.append([full[8 * i : 8 * i + 8] for i in range(R // 8)])
    lane8, row8 = lanes((8, 128)), rows((8, 1))
    scale = [jnp.zeros((8, 128), f32)]
    for k in range(0, R, 8):
        for s in range(1):
            scale[s] = eliminate(blocks[s], scale[s], k, 8, lane8, row8)
    for s in range(1):
        w = jnp.concatenate(blocks[s], axis=0)
        w = jnp.where(lane == row, 1.0, jnp.where(lane < row, w, 0.0))
        inv = jnp.sum(jnp.where(lane == row, scale[s][0:1], 0.0), axis=1, keepdims=True)
        out_ref[s] = dot(w[:, 0:R], w * inv, ((0,), (0,)))


def solve(m_ref, own_ref, *refs):
    inverses, (out_ref, raw_ref) = [ref[0] for ref in refs[:S]], refs[S:]
    count = m_ref.shape[0]
    squares = []
    for s in range(S):
        inv = pick(start_of() ^ s, inverses)
        both = jnp.concatenate([m_ref[:, s, 0:R], own_ref[0:8, s, 0:R]], axis=0)
        raw = dot(both, inv, ((1,), (0,)))
        squares.append(jnp.sum(raw[0:count] * raw[0:count], axis=0, keepdims=True))
        raw_ref[s : s + 1, :] = raw[count : count + 1]
    total = jnp.concatenate(squares, axis=0)
    out_ref[...] = jnp.broadcast_to(total[None], out_ref.shape)


def finish_of(row_total):
    def finish(got_ref, raw_ref, fa_ref, w_ref):
        total = jnp.sum(got_ref[...], axis=0)
        weights = jnp.sqrt(total / row_total + 1e-06)
        w_ref[...] = weights[:, 0:R]
        fa_ref[0] = (raw_ref[...] / weights)[:, 0:R]

    return finish


def shards(tensor, factor_b, factor_c):
    ni = tensor.shape[0]
    ia, ja, ka = (lax.axis_size(a) for a in ("ia", "ja", "ka"))
    nb, nc = factor_b.shape[0], factor_c.shape[0]
    cost = pl.CostEstimate(flops=int(1e10), bytes_accessed=int(4e7), transcendentals=0)
    slots_c, b_flat = call(
        prepare,
        [(ja, 3 * nc + 16, 128), (nb, W)],
        cost=cost,
        scratch=[pltpu.VMEM(factor_b.shape, f32), pltpu.VMEM(factor_c.shape, f32), pltpu.SemaphoreType.DMA((2,))],
        hbm=2,
        limit=56,
    )(factor_b, factor_c)
    got_c = lax.all_to_all(slots_c, "ja", 0, 0)
    b_block = lax.all_gather(b_flat, "ka", axis=0, tiled=True)
    slots_m = call(contract, [(ja * ka, 16, 128)], scratch=[pltpu.VMEM((ni, W), f32)])(tensor, got_c, b_block)[0]
    got_m = lax.all_to_all(slots_m, ("ja", "ka"), 0, 0)
    own = call(own_row, [(ja * ka, S, 128)])(got_m)[0]
    all_rows = lax.all_to_all(own, ("ja", "ka"), 0, 0)
    inverse = call(invert, [(1, R, 128)], cost=cost, scratch=[pltpu.VMEM((R, 128), f32)])(got_m)[0]
    others = [lax.ppermute(inverse, "ia", [(n, n ^ d) for n in range(ia)]) for d in range(1, S)]
    squares, raw = call(solve, [(ia, S, 128), (S, 128)])(all_rows, own, inverse, *others)
    got_s = lax.all_to_all(squares, "ia", 0, 0)
    return tuple(call(finish_of(ni * ia), [(1, S, R), (S, R)])(got_s, raw))


def solution(mesh):
    in_specs = (P("ia", "ja", "ka"), P(("ja", "ka"), None, None), P(("ka", "ja"), None, None))
    out_specs = (P(("ia", "ja", "ka"), None, None), P())
    return jax.shard_map(shards, mesh=mesh, in_specs=in_specs, out_specs=out_specs, check_vma=False)
```

```python
import jax
import jax.numpy as jnp
from jax import lax
from jax.experimental import pallas as pl
from jax.experimental.pallas import tpu as pltpu
from jax.sharding import PartitionSpec as P

highest = lax.Precision.HIGHEST
f32 = jnp.float32
bf16 = jnp.bfloat16

R = 96
S = 4
W = S * R
VMEM = pl.BlockSpec(memory_space=pltpu.VMEM)
HBM = pl.BlockSpec(memory_space=pltpu.HBM)


def dot(a, b, dims, precision=highest):
    return lax.dot_general(a, b, (dims, ((), ())), precision=precision, preferred_element_type=f32)


def lanes(shape):
    return lax.broadcasted_iota(jnp.int32, shape, 1)


def rows(shape):
    return lax.broadcasted_iota(jnp.int32, shape, 0)


def call(body, out, cost=None, scratch=(), hbm=0, limit=32):
    shapes = [jax.ShapeDtypeStruct(o, f32) for o in out]

    def run(*args):
        return pl.pallas_call(
            body,
            out_shape=shapes,
            in_specs=[HBM] * hbm + [VMEM] * (len(args) - hbm),
            out_specs=[VMEM] * len(shapes),
            scratch_shapes=list(scratch),
            compiler_params=pltpu.CompilerParams(vmem_limit_bytes=limit * 1024 * 1024),
            cost_estimate=cost,
        )(*args)

    return run


def start_of():
    return lax.rem(lax.axis_index("ia"), S)


def pick(which, choices):
    out = choices[0]
    for n in range(1, len(choices)):
        out = jnp.where(which == n, choices[n], out)
    return out


def prepare(fb_hbm, fc_hbm, out_ref, b_ref, fb_ref, fc_ref, sems):
    copy_b = pltpu.make_async_copy(fb_hbm, fb_ref, sems.at[0])
    copy_c = pltpu.make_async_copy(fc_hbm, fc_ref, sems.at[1])
    copy_b.start()
    copy_c.start()
    copy_b.wait()
    copy_c.wait()
    peers, nc = out_ref.shape[0], fc_ref.shape[0]
    b = pick(start_of(), [fb_ref[:, s, :] for s in range(S)])
    c = pick(start_of(), [fc_ref[:, s, :] for s in range(S)])
    wide_b = jnp.concatenate([b, jnp.zeros((b.shape[0], 128 - R), f32)], axis=1)
    wide_c = jnp.concatenate([c, jnp.zeros((c.shape[0], 128 - R), f32)], axis=1)
    gram_b = dot(b, wide_b, ((0,), (0,)))
    gram_c = dot(c, pltpu.roll(wide_c, 1, 1), ((0,), (0,)))
    z = jnp.where(lanes((R, 128)) <= rows((R, 128)), gram_b, gram_c)
    c_flat = jnp.concatenate([fc_ref[:, s, :] for s in range(S)], axis=1)
    b_ref[...] = jnp.concatenate([fb_ref[:, s, :] for s in range(S)], axis=1)
    depth = R // peers
    fill = jnp.zeros((out_ref.shape[1] - 3 * nc - depth, 128), f32)
    for p in range(peers):
        for q in range(3):
            out_ref[p, q * nc : (q + 1) * nc, :] = c_flat[:, q * 128 : (q + 1) * 128]
        out_ref[p, 3 * nc :, :] = jnp.concatenate([z[p * depth : (p + 1) * depth], fill], axis=0)


def gathered(ref, count):
    pieces = [ref[:, q * count : (q + 1) * count, :].reshape(ref.shape[0] * count, 128) for q in range(3)]
    return jnp.concatenate(pieces, axis=1)


def contract(t_ref, c_got_ref, b_ref, out_ref, m_ref):
    ni, nj, nk = t_ref.shape
    nc = nk // c_got_ref.shape[0]
    c = gathered(c_got_ref, nc)
    b = b_ref[...]
    c_high = c.astype(bf16)
    c_low = (c - c_high.astype(f32)).astype(bf16)
    parts = jnp.concatenate([c_high, c_high, c_low], axis=0)
    group = 8
    for at in range(0, ni, group):
        t = t_ref[at : at + group, :, :].reshape(group * nj, nk)
        t_high = t.astype(bf16)
        t_low = (t - t_high.astype(f32)).astype(bf16)
        value = dot(jnp.concatenate([t_high, t_low, t_high], axis=1), parts, ((1,), (0,)), None)
        m_ref[at : at + group, :] = jnp.sum(value.reshape(group, nj, W) * b[None], axis=1)
    share = jnp.sum(c_got_ref[:, 3 * nc :, :], axis=0)
    out_ref[...] = jnp.broadcast_to(share[None], out_ref.shape)
    for q in range(3):
        out_ref[:, 12 + q, :] = m_ref[:, q * 128 : (q + 1) * 128]


def own_row(got_ref, out_ref):
    total = jnp.sum(got_ref[:, 8:16, :], axis=0)
    flat = jnp.concatenate([total[4 + q : 5 + q] for q in range(3)], axis=1)
    pad = jnp.zeros((1, 128 - R), f32)
    row = [jnp.concatenate([flat[:, s * R : (s + 1) * R], pad], axis=1) for s in range(S)]
    out_ref[...] = jnp.broadcast_to(jnp.concatenate(row, axis=0)[None], out_ref.shape)


def wide(v):
    return jnp.broadcast_to(v, (8, 128))


def eliminate(blocks, scale, k, q, lane8, row8):
    own, m = divmod(k, 8)
    hit = (lane8 >= k) & (lane8 < k + q)
    mine = blocks[own]
    row = [wide(mine[m + p : m + p + 1]) for p in range(q)]
    cols = [wide(mine[:, k + j : k + j + 1]) for j in range(q)]
    a = {(p, j): wide(cols[j][m + p : m + p + 1]) for p in range(q) for j in range(p, q)}
    inv, u, unit = [], {}, []
    for p in range(q):
        inv.append(1.0 / a[p, p])
        unit.append(jnp.where(lane8 == k + p, 1.0, row[p]))
        scale = jnp.where(lane8 == k + p, inv[p], scale)
        for i in range(p + 1, q):
            u[i, p] = a[p, i] * inv[p]
            for j in range(i, q):
                a[i, j] = a[i, j] - u[i, p] * a[p, j]
        for i in range(p + 1, q):
            row[i] = jnp.where(lane8 == k + p, 0.0, row[i]) - u[i, p] * unit[p]
    steps = [None] * q
    for p in reversed(range(q)):
        step = jnp.where((lane8 > k + p) & hit, 0.0, unit[p]) * inv[p]
        for j in range(p + 1, q):
            step = step - u[j, p] * steps[j]
        steps[p] = step
    for i in range(own, len(blocks)):
        old = blocks[i]
        new = jnp.where(hit, 0.0, old)
        for p in range(q):
            new = new - wide(old[:, k + p : k + p + 1]) * steps[p]
        if i == own:
            new = jnp.where(row8 >= m + q, new, old)
            for p in range(1, q):
                new = jnp.where(row8 == m + p, row[p], new)
        blocks[i] = new
    return scale


def invert(got_ref, out_ref, z_ref):
    ka = lax.axis_size("ka")
    for p in range(got_ref.shape[0] // ka):
        z_ref[12 * p : 12 * (p + 1), :] = jnp.sum(got_ref[ka * p : ka * (p + 1), 0:12, :], axis=0)
    lane, row = lanes((R, 128)), rows((R, 128))
    fill = jnp.zeros((128 - R, 128), f32)
    blocks = []
    for s in range(1):
        z = z_ref[s * R : (s + 1) * R, :]
        low = jnp.where(lane <= row, z, 0.0)
        b_up = jnp.concatenate([low, fill], axis=0).T[0:R]
        c_up = pltpu.roll(z, 127, 1)
        up = jnp.where((lane >= row) & (lane < R), b_up * c_up, 0.0)
        strict = jnp.where(lane > row, up, 0.0)
        full = up + jnp.concatenate([strict, fill], axis=0).T[0:R]
        blocks.append([full[8 * i : 8 * i + 8] for i in range(R // 8)])
    lane8, row8 = lanes((8, 128)), rows((8, 1))
    scale = [jnp.zeros((8, 128), f32)]
    for k in range(0, R, 8):
        for s in range(1):
            scale[s] = eliminate(blocks[s], scale[s], k, 8, lane8, row8)
    for s in range(1):
        w = jnp.concatenate(blocks[s], axis=0)
        w = jnp.where(lane == row, 1.0, jnp.where(lane < row, w, 0.0))
        inv = jnp.sum(jnp.where(lane == row, scale[s][0:1], 0.0), axis=1, keepdims=True)
        out_ref[s] = dot(w[:, 0:R], w * inv, ((0,), (0,)))


def solve(m_ref, own_ref, *refs):
    inverses, (out_ref, raw_ref) = [ref[0] for ref in refs[:S]], refs[S:]
    count = m_ref.shape[0]
    squares = []
    for s in range(S):
        inv = pick(start_of() ^ s, inverses)
        both = jnp.concatenate([m_ref[:, s, 0:R], own_ref[0:8, s, 0:R]], axis=0)
        raw = dot(both, inv, ((1,), (0,)))
        squares.append(jnp.sum(raw[0:count] * raw[0:count], axis=0, keepdims=True))
        raw_ref[s : s + 1, :] = raw[count : count + 1]
    total = jnp.concatenate(squares, axis=0)
    out_ref[...] = jnp.broadcast_to(total[None], out_ref.shape)


def finish_of(row_total):
    def finish(got_ref, raw_ref, fa_ref, w_ref):
        total = jnp.sum(got_ref[...], axis=0)
        weights = jnp.sqrt(total / row_total + 1e-06)
        w_ref[...] = weights[:, 0:R]
        fa_ref[0] = (raw_ref[...] / weights)[:, 0:R]

    return finish


def shards(tensor, factor_b, factor_c):
    ni = tensor.shape[0]
    ia, ja, ka = (lax.axis_size(a) for a in ("ia", "ja", "ka"))
    nb, nc = factor_b.shape[0], factor_c.shape[0]
    cost = pl.CostEstimate(flops=int(1e10), bytes_accessed=int(4e7), transcendentals=0)
    slots_c, b_flat = call(
        prepare,
        [(ja, 3 * nc + 16, 128), (nb, W)],
        cost=cost,
        scratch=[pltpu.VMEM(factor_b.shape, f32), pltpu.VMEM(factor_c.shape, f32), pltpu.SemaphoreType.DMA((2,))],
        hbm=2,
        limit=56,
    )(factor_b, factor_c)
    got_c = lax.all_to_all(slots_c, "ja", 0, 0)
    b_block = lax.all_gather(b_flat, "ka", axis=0, tiled=True)
    slots_m = call(contract, [(ja * ka, 16, 128)], scratch=[pltpu.VMEM((ni, W), f32)])(tensor, got_c, b_block)[0]
    got_m = lax.all_to_all(slots_m, ("ja", "ka"), 0, 0)
    own = call(own_row, [(ja * ka, S, 128)])(got_m)[0]
    all_rows = lax.all_to_all(own, ("ja", "ka"), 0, 0)
    inverse = call(invert, [(1, R, 128)], cost=cost, scratch=[pltpu.VMEM((R, 128), f32)])(got_m)[0]
    others = [lax.ppermute(inverse, "ia", [(n, n ^ d) for n in range(ia)]) for d in range(1, S)]
    squares, raw = call(solve, [(ia, S, 128), (S, 128)])(all_rows, own, inverse, *others)
    got_s = lax.all_to_all(squares, "ia", 0, 0)
    return tuple(call(finish_of(ni * ia), [(1, S, R), (S, R)])(got_s, raw))


def solution(mesh):
    in_specs = (P("ia", "ja", "ka"), P(("ja", "ka"), None, None), P(("ka", "ja"), None, None))
    out_specs = (P(("ia", "ja", "ka"), None, None), P())
    return jax.shard_map(shards, mesh=mesh, in_specs=in_specs, out_specs=out_specs, check_vma=False)
```

```python
import jax
import jax.numpy as jnp
from jax import lax
from jax.experimental import pallas as pl
from jax.experimental.pallas import tpu as pltpu
from jax.sharding import PartitionSpec as P

highest = lax.Precision.HIGHEST
f32 = jnp.float32
bf16 = jnp.bfloat16

R = 96
S = 4
W = S * R
VMEM = pl.BlockSpec(memory_space=pltpu.VMEM)
HBM = pl.BlockSpec(memory_space=pltpu.HBM)


def dot(a, b, dims, precision=highest):
    return lax.dot_general(a, b, (dims, ((), ())), precision=precision, preferred_element_type=f32)


def lanes(shape):
    return lax.broadcasted_iota(jnp.int32, shape, 1)


def rows(shape):
    return lax.broadcasted_iota(jnp.int32, shape, 0)


def call(body, out, cost=None, scratch=(), hbm=0, limit=32):
    shapes = [jax.ShapeDtypeStruct(o, f32) for o in out]

    def run(*args):
        return pl.pallas_call(
            body,
            out_shape=shapes,
            in_specs=[HBM] * hbm + [VMEM] * (len(args) - hbm),
            out_specs=[VMEM] * len(shapes),
            scratch_shapes=list(scratch),
            compiler_params=pltpu.CompilerParams(vmem_limit_bytes=limit * 1024 * 1024),
            cost_estimate=cost,
        )(*args)

    return run


def start_of():
    return lax.rem(lax.axis_index("ia"), S)


def pick(which, choices):
    out = choices[0]
    for n in range(1, len(choices)):
        out = jnp.where(which == n, choices[n], out)
    return out


def prepare(fb_hbm, fc_hbm, out_ref, b_ref, fb_ref, fc_ref, sems):
    copy_b = pltpu.make_async_copy(fb_hbm, fb_ref, sems.at[0])
    copy_c = pltpu.make_async_copy(fc_hbm, fc_ref, sems.at[1])
    copy_c.start()
    copy_b.start()
    copy_c.wait()
    peers, nc = out_ref.shape[0], fc_ref.shape[0]
    c_flat = jnp.concatenate([fc_ref[:, s, :] for s in range(S)], axis=1)
    for p in range(peers):
        for q in range(3):
            out_ref[p, q * nc : (q + 1) * nc, :] = c_flat[:, q * 128 : (q + 1) * 128]
    copy_b.wait()
    b = pick(start_of(), [fb_ref[:, s, :] for s in range(S)])
    c = pick(start_of(), [fc_ref[:, s, :] for s in range(S)])
    wide_b = jnp.concatenate([b, jnp.zeros((b.shape[0], 128 - R), f32)], axis=1)
    wide_c = jnp.concatenate([c, jnp.zeros((c.shape[0], 128 - R), f32)], axis=1)
    gram_b = dot(b, wide_b, ((0,), (0,)))
    gram_c = dot(c, pltpu.roll(wide_c, 1, 1), ((0,), (0,)))
    z = jnp.where(lanes((R, 128)) <= rows((R, 128)), gram_b, gram_c)
    b_ref[...] = jnp.concatenate([fb_ref[:, s, :] for s in range(S)], axis=1)
    depth = R // peers
    fill = jnp.zeros((out_ref.shape[1] - 3 * nc - depth, 128), f32)
    for p in range(peers):
        out_ref[p, 3 * nc :, :] = jnp.concatenate([z[p * depth : (p + 1) * depth], fill], axis=0)


def gathered(ref, count):
    pieces = [ref[:, q * count : (q + 1) * count, :].reshape(ref.shape[0] * count, 128) for q in range(3)]
    return jnp.concatenate(pieces, axis=1)


def contract(t_ref, c_got_ref, b_ref, out_ref, m_ref):
    ni, nj, nk = t_ref.shape
    nc = nk // c_got_ref.shape[0]
    c = gathered(c_got_ref, nc)
    b = b_ref[...]
    c_high = c.astype(bf16)
    c_low = (c - c_high.astype(f32)).astype(bf16)
    twice = jnp.concatenate([c_high, c_high], axis=0)
    group = 8
    for at in range(0, ni, group):
        t = t_ref[at : at + group, :, :].reshape(group * nj, nk)
        t_high = t.astype(bf16)
        t_low = (t - t_high.astype(f32)).astype(bf16)
        both = jnp.concatenate([t_high, t_low], axis=1)
        value = dot(both, twice, ((1,), (0,)), None) + dot(t_high, c_low, ((1,), (0,)), None)
        m_ref[at : at + group, :] = jnp.sum(value.reshape(group, nj, W) * b[None], axis=1)
    share = jnp.sum(c_got_ref[:, 3 * nc :, :], axis=0)
    out_ref[...] = jnp.broadcast_to(share[None], out_ref.shape)
    for q in range(3):
        out_ref[:, 12 + q, :] = m_ref[:, q * 128 : (q + 1) * 128]


def own_row(got_ref, out_ref):
    total = jnp.sum(got_ref[:, 8:16, :], axis=0)
    flat = jnp.concatenate([total[4 + q : 5 + q] for q in range(3)], axis=1)
    pad = jnp.zeros((1, 128 - R), f32)
    row = [jnp.concatenate([flat[:, s * R : (s + 1) * R], pad], axis=1) for s in range(S)]
    out_ref[...] = jnp.broadcast_to(jnp.concatenate(row, axis=0)[None], out_ref.shape)


def wide(v):
    return jnp.broadcast_to(v, (8, 128))


def eliminate(blocks, scale, k, q, lane8, row8):
    own, m = divmod(k, 8)
    hit = (lane8 >= k) & (lane8 < k + q)
    mine = blocks[own]
    row = [wide(mine[m + p : m + p + 1]) for p in range(q)]
    cols = [wide(mine[:, k + j : k + j + 1]) for j in range(q)]
    a = {(p, j): wide(cols[j][m + p : m + p + 1]) for p in range(q) for j in range(p, q)}
    inv, u, unit = [], {}, []
    for p in range(q):
        inv.append(1.0 / a[p, p])
        unit.append(jnp.where(lane8 == k + p, 1.0, row[p]))
        scale = jnp.where(lane8 == k + p, inv[p], scale)
        for i in range(p + 1, q):
            u[i, p] = a[p, i] * inv[p]
            for j in range(i, q):
                a[i, j] = a[i, j] - u[i, p] * a[p, j]
        for i in range(p + 1, q):
            row[i] = jnp.where(lane8 == k + p, 0.0, row[i]) - u[i, p] * unit[p]
    steps = [None] * q
    for p in reversed(range(q)):
        step = jnp.where((lane8 > k + p) & hit, 0.0, unit[p]) * inv[p]
        for j in range(p + 1, q):
            step = step - u[j, p] * steps[j]
        steps[p] = step
    for i in range(own, len(blocks)):
        old = blocks[i]
        new = jnp.where(hit, 0.0, old)
        for p in range(q):
            new = new - wide(old[:, k + p : k + p + 1]) * steps[p]
        if i == own:
            new = jnp.where(row8 >= m + q, new, old)
            for p in range(1, q):
                new = jnp.where(row8 == m + p, row[p], new)
        blocks[i] = new
    return scale


def invert(got_ref, out_ref, z_ref):
    ka = lax.axis_size("ka")
    for p in range(got_ref.shape[0] // ka):
        z_ref[12 * p : 12 * (p + 1), :] = jnp.sum(got_ref[ka * p : ka * (p + 1), 0:12, :], axis=0)
    lane, row = lanes((R, 128)), rows((R, 128))
    fill = jnp.zeros((128 - R, 128), f32)
    blocks = []
    for s in range(1):
        z = z_ref[s * R : (s + 1) * R, :]
        low = jnp.where(lane <= row, z, 0.0)
        b_up = jnp.concatenate([low, fill], axis=0).T[0:R]
        c_up = pltpu.roll(z, 127, 1)
        up = jnp.where((lane >= row) & (lane < R), b_up * c_up, 0.0)
        strict = jnp.where(lane > row, up, 0.0)
        full = up + jnp.concatenate([strict, fill], axis=0).T[0:R]
        blocks.append([full[8 * i : 8 * i + 8] for i in range(R // 8)])
    lane8, row8 = lanes((8, 128)), rows((8, 1))
    scale = [jnp.zeros((8, 128), f32)]
    for k in range(0, R, 8):
        for s in range(1):
            scale[s] = eliminate(blocks[s], scale[s], k, 8, lane8, row8)
    for s in range(1):
        w = jnp.concatenate(blocks[s], axis=0)
        w = jnp.where(lane == row, 1.0, jnp.where(lane < row, w, 0.0))
        inv = jnp.sum(jnp.where(lane == row, scale[s][0:1], 0.0), axis=1, keepdims=True)
        out_ref[s] = dot(w[:, 0:R], w * inv, ((0,), (0,)))


def solve(m_ref, own_ref, *refs):
    inverses, (out_ref, raw_ref) = [ref[0] for ref in refs[:S]], refs[S:]
    count = m_ref.shape[0]
    squares = []
    for s in range(S):
        inv = pick(start_of() ^ s, inverses)
        both = jnp.concatenate([m_ref[:, s, 0:R], own_ref[0:8, s, 0:R]], axis=0)
        raw = dot(both, inv, ((1,), (0,)))
        squares.append(jnp.sum(raw[0:count] * raw[0:count], axis=0, keepdims=True))
        raw_ref[s : s + 1, :] = raw[count : count + 1]
    total = jnp.concatenate(squares, axis=0)
    out_ref[...] = jnp.broadcast_to(total[None], out_ref.shape)


def finish_of(row_total):
    def finish(got_ref, raw_ref, fa_ref, w_ref):
        total = jnp.sum(got_ref[...], axis=0)
        weights = jnp.sqrt(total / row_total + 1e-06)
        w_ref[...] = weights[:, 0:R]
        fa_ref[0] = (raw_ref[...] / weights)[:, 0:R]

    return finish


def shards(tensor, factor_b, factor_c):
    ni = tensor.shape[0]
    ia, ja, ka = (lax.axis_size(a) for a in ("ia", "ja", "ka"))
    nb, nc = factor_b.shape[0], factor_c.shape[0]
    cost = pl.CostEstimate(flops=int(1e10), bytes_accessed=int(4e7), transcendentals=0)
    slots_c, b_flat = call(
        prepare,
        [(ja, 3 * nc + 16, 128), (nb, W)],
        cost=cost,
        scratch=[pltpu.VMEM(factor_b.shape, f32), pltpu.VMEM(factor_c.shape, f32), pltpu.SemaphoreType.DMA((2,))],
        hbm=2,
        limit=56,
    )(factor_b, factor_c)
    got_c = lax.all_to_all(slots_c, "ja", 0, 0)
    b_block = lax.all_gather(b_flat, "ka", axis=0, tiled=True)
    slots_m = call(contract, [(ja * ka, 16, 128)], scratch=[pltpu.VMEM((ni, W), f32)])(tensor, got_c, b_block)[0]
    got_m = lax.all_to_all(slots_m, ("ja", "ka"), 0, 0)
    own = call(own_row, [(ja * ka, S, 128)])(got_m)[0]
    all_rows = lax.all_to_all(own, ("ja", "ka"), 0, 0)
    inverse = call(invert, [(1, R, 128)], cost=cost, scratch=[pltpu.VMEM((R, 128), f32)])(got_m)[0]
    others = [lax.ppermute(inverse, "ia", [(n, n ^ d) for n in range(ia)]) for d in range(1, S)]
    squares, raw = call(solve, [(ia, S, 128), (S, 128)])(all_rows, own, inverse, *others)
    got_s = lax.all_to_all(squares, "ia", 0, 0)
    return tuple(call(finish_of(ni * ia), [(1, S, R), (S, R)])(got_s, raw))


def solution(mesh):
    in_specs = (P("ia", "ja", "ka"), P(("ja", "ka"), None, None), P(("ka", "ja"), None, None))
    out_specs = (P(("ia", "ja", "ka"), None, None), P())
    return jax.shard_map(shards, mesh=mesh, in_specs=in_specs, out_specs=out_specs, check_vma=False)
```
